256 devices in a mesh: lon: 32 (over z, y_lo, core), lat: 8 (over y_hi, x).
Axes of the slice: x: 4, y: 4 (y_hi: 2, y_lo: 2; y = y_hi * 2 + y_lo), z: 8, core: 2. Of those that a mesh axis runs over, the one named last changes fastest.
Arguments:
- patches: bfloat16 [64, 1024, 1104], P('lat', 'lon'), may hold values from -6 to 6
- embed_weight: bfloat16 [1104, 768], replicated, may hold values from -0.1875 to 0.1875
- embed_bias: float32 [768], replicated, may hold values from -3 to 3
- conv_weight: bfloat16 [3, 3, 768, 768], P(None, None, None, 'lat'), may hold values from -0.078125 to 0.078125
- conv_bias: float32 [768], replicated, may hold values from -3 to 3
- norm_gain: float32 [768], replicated, may hold values from 0.1 to 1.9
- up_weight: bfloat16 [768, 3072], P(None, 'lon'), may hold values from -0.21875 to 0.21875
- up_bias: float32 [1, 3072], P(None, 'lon'), may hold values from -3 to 3
- down_weight: bfloat16 [768, 3072], P(None, 'lon'), may hold values from -0.109375 to 0.109375
- down_bias: float32 [768], replicated, may hold values from -3 to 3
Outputs:
- features: bfloat16 [64, 1024, 768], P('lat', 'lon')
The draws below stay inside these ranges and needn't reach their ends.
All inputs are finite; a program needn't handle non-finite values.
Results may differ from the reference program's by a relative error of at most 0.022.
Values may be sent and summed in bfloat16 or wider, within the bound.
A program may use at most 128 MiB of HBM per device.

```python
import jax
import jax.numpy as jnp
from jax import lax

WIDTH = 768
HIDDEN_SIZE = 3072
PATCH_IN = 1104
NLAT = 64
NLON = 1024
N_LON = 32


def steps_of(key, dims, split, low, largest):
    loudness = 1.0
    for dim, parts in split:
        heights = jax.random.uniform(jax.random.fold_in(jax.random.fold_in(key, 6), dim), (parts,), jnp.float32, low / len(split), largest / len(split))
        loudness = loudness * jnp.repeat(jnp.exp(heights), dims[dim] // parts).reshape((-1,) + (1,) * (len(dims) - 1 - dim))
    return loudness


def centred(own_key, extent, deviation, most, pieces=(), kind=jnp.bfloat16):
    gain = steps_of(own_key, extent, pieces, -0.22, 0.18) if pieces else 1.0
    result = jax.random.normal(own_key, extent, jnp.float32) * deviation * gain
    return jnp.minimum(jnp.maximum(result, -most), most).astype(kind)


def setup_inputs(seed: int = 0) -> dict:
    key_list = jax.random.split(jax.random.key(seed), 11)
    patches = centred(key_list[0], (NLAT, NLON, PATCH_IN), 1.0, 6.0, ((0, 8), (1, 32)))
    embed_weight = centred(key_list[1], (PATCH_IN, WIDTH), PATCH_IN ** -0.5, 0.1875)
    embed_bias = centred(key_list[2], (WIDTH,), 0.5, 3.0, (), jnp.float32)
    conv_weight = centred(key_list[3], (3, 3, WIDTH, WIDTH), (9 * WIDTH) ** -0.5, 0.078125, ((3, 8),))
    conv_bias = centred(key_list[4], (WIDTH,), 0.5, 3.0, (), jnp.float32)
    norm_gain = jnp.clip(1.0 + 0.18 * jax.random.normal(key_list[5], (WIDTH,), jnp.float32), 0.1, 1.9)
    up_weight = centred(key_list[6], (WIDTH, HIDDEN_SIZE), WIDTH ** -0.5, 0.21875, ((1, 32),))
    up_bias = centred(key_list[7], (1, HIDDEN_SIZE), 0.5, 3.0, ((1, 32),), jnp.float32)
    down_weight = centred(key_list[8], (WIDTH, HIDDEN_SIZE), HIDDEN_SIZE ** -0.5, 0.109375, ((1, 32),))
    down_bias = centred(key_list[9], (WIDTH,), 0.5, 3.0, (), jnp.float32)
    return dict(patches=patches, embed_weight=embed_weight, embed_bias=embed_bias, conv_weight=conv_weight, conv_bias=conv_bias, norm_gain=norm_gain, up_weight=up_weight, up_bias=up_bias, down_weight=down_weight, down_bias=down_bias)


def reference(patches, embed_weight, embed_bias, conv_weight, conv_bias, norm_gain, up_weight, up_bias, down_weight, down_bias):
    flat_in = patches.reshape(NLAT * NLON, PATCH_IN)
    embedded = (jnp.dot(flat_in, embed_weight, preferred_element_type=jnp.float32) + embed_bias).astype(jnp.bfloat16)
    embedded = embedded.reshape(NLAT, NLON, WIDTH)
    activated = jax.nn.gelu(embedded.astype(jnp.float32)).astype(jnp.bfloat16)
    wrapped = jnp.concatenate([activated[:, -1:], activated, activated[:, :1]], axis=1)
    padded = jnp.pad(wrapped, ((1, 1), (0, 0), (0, 0)))
    convolved = jnp.zeros((NLAT * NLON, WIDTH), jnp.float32)
    for row_off in range(3):
        for col_off in range(3):
            window = padded[row_off:row_off + NLAT, col_off:col_off + NLON].reshape(NLAT * NLON, WIDTH)
            convolved = convolved + jnp.dot(window, conv_weight[row_off, col_off], preferred_element_type=jnp.float32)
    mixed = (embedded.reshape(NLAT * NLON, WIDTH).astype(jnp.float32) + convolved + conv_bias).astype(jnp.bfloat16)
    values = mixed.astype(jnp.float32)
    center = lax.optimization_barrier(jnp.mean(values, axis=1, keepdims=True))
    spread = lax.optimization_barrier(jnp.mean((values - center) ** 2, axis=1, keepdims=True))
    normed = ((values - center) * lax.rsqrt(spread + 1e-05) * norm_gain).astype(jnp.bfloat16)
    units = HIDDEN_SIZE // N_LON

    def one_block(total, index):
        start = index * units
        up_block = lax.dynamic_slice_in_dim(up_weight, start, units, 1)
        bias_block = lax.dynamic_slice_in_dim(up_bias, start, units, 1)
        down_block = lax.dynamic_slice_in_dim(down_weight, start, units, 1)
        hidden = jax.nn.gelu(jnp.dot(normed, up_block, preferred_element_type=jnp.float32) + bias_block).astype(jnp.bfloat16)
        partial_out = lax.dot_general(hidden, down_block, (((1,), (1,)), ((), ())), preferred_element_type=jnp.float32)
        partial_out = lax.optimization_barrier(partial_out.astype(jnp.bfloat16)).astype(jnp.float32)
        return (total + partial_out, None)
    summed, _ = lax.scan(one_block, jnp.zeros((NLAT * NLON, WIDTH), jnp.float32), jnp.arange(N_LON, dtype=jnp.int32))
    features = (values + summed + down_bias).astype(jnp.bfloat16)
    return features.reshape(NLAT, NLON, WIDTH)
```

```python
import jax
import jax.numpy as jnp
from jax import lax
from jax.sharding import PartitionSpec as P


def extended(value, sides, width, wrap):
    for axis, dim in sides:
        size, length = (lax.axis_size(axis), value.shape[dim])
        up = [(i, (i + 1) % size) for i in range(size if wrap else size - 1)]
        down = [(j, i) for i, j in up]
        last = lax.slice_in_dim(value, length - width, length, axis=dim)
        leading = lax.slice_in_dim(value, 0, width, axis=dim)
        before = lax.ppermute(last, axis, up)
        after = lax.ppermute(leading, axis, down)
        value = jnp.concatenate([before, value, after], axis=dim)
    return value


def stencil(framed, kernel, rows, cols, width):
    total = jnp.zeros((rows * cols, kernel.shape[3]), jnp.float32)
    for row_off in range(3):
        for col_off in range(3):
            window = framed[row_off : row_off + rows, col_off : col_off + cols].reshape(
                rows * cols, width
            )
            total = total + jnp.dot(
                window, kernel[row_off, col_off], preferred_element_type=jnp.float32
            )
    return total.reshape(rows, cols, kernel.shape[3])


def body(
    patches,
    embed_weight,
    embed_bias,
    conv_weight,
    conv_bias,
    norm_gain,
    up_weight,
    up_bias,
    down_weight,
    down_bias,
):
    rows, cols, inputs = patches.shape
    width = embed_weight.shape[1]
    embedded = (
        jnp.dot(
            patches.reshape(rows * cols, inputs), embed_weight, preferred_element_type=jnp.float32
        )
        + embed_bias
    ).astype(jnp.bfloat16)
    embedded = embedded.reshape(rows, cols, width)
    activated = jax.nn.gelu(embedded.astype(jnp.float32)).astype(jnp.bfloat16)
    widened = extended(activated, (("lon", 1),), 1, True)
    framed = extended(widened, (("lat", 0),), 1, False)
    convolved = stencil(
        framed, lax.all_gather(conv_weight, "lat", axis=3, tiled=True), rows, cols, width
    )
    mixed = (embedded.astype(jnp.float32) + convolved + conv_bias).astype(jnp.bfloat16)
    values = mixed.astype(jnp.float32)
    center = jnp.mean(values, axis=2, keepdims=True)
    spread = jnp.mean((values - center) ** 2, axis=2, keepdims=True)
    normed = ((values - center) * lax.rsqrt(spread + 1e-05) * norm_gain).astype(jnp.bfloat16)
    up_all = lax.all_gather(up_weight.T, "lon", axis=0, tiled=True)
    bias_all = lax.all_gather(up_bias, "lon", axis=1, tiled=True)
    down_all = lax.all_gather(down_weight.T, "lon", axis=0, tiled=True)
    flat_tokens = normed.reshape(rows * cols, width)
    hidden = jax.nn.gelu(
        lax.dot_general(
            flat_tokens, up_all, (((1,), (1,)), ((), ())), preferred_element_type=jnp.float32
        )
        + bias_all
    ).astype(jnp.bfloat16)
    result = jnp.dot(hidden, down_all, preferred_element_type=jnp.float32)
    return (values + result.reshape(rows, cols, width) + down_bias).astype(jnp.bfloat16)


def solution(mesh):
    in_specs = (
        P("lat", "lon", None),
        P(),
        P(),
        P(None, None, None, "lat"),
        P(),
        P(),
        P(None, "lon"),
        P(None, "lon"),
        P(None, "lon"),
        P(),
    )
    out_specs = P("lat", "lon", None)
    return jax.shard_map(body, mesh=mesh, in_specs=in_specs, out_specs=out_specs, check_vma=False)
```

```python
import functools

import jax
import jax.numpy as jnp
from jax import lax
from jax.experimental import pallas as pl
from jax.experimental.pallas import tpu as pltpu
from jax.sharding import PartitionSpec as P

MESH = pl.DeviceIdType.MESH
NX, NZ = 4, 8
ROWS, COLS, WIDTH, UNITS = 8, 32, 768, 96
TOKENS, HALF, TILE = ROWS * COLS, UNITS // 2, 256
TAPS = 9
Y_FIRST = (0, 0, 1, 1, 1, 0, 0, 1, 1)
WAY = (-1, -1, 1, -1, 1, 1, -1, -1, 1)
ORDER = (
    ("own", 0), ("own", 1), ("own", 2), ("own", 3), ("own", 4), ("mlp",), ("embed",), ("near", 0), ("near", 1), ("own", 5),
    ("own", 6), ("mlp_y",), ("across", 2), ("share_up", 0), ("across", 3), ("own", 7), ("share_down", 0), ("across", 4), ("down", 1, "p"),
    ("down", 1, "m"), ("far", 0), ("own", 8), ("up", 1, "p"), ("up", 1, "m"), ("far", 1), ("share_up", 1, "p"), ("share_up", 1, "m"),
    ("share_down", 1, "p"), ("near", 5), ("down", 2, "p"), ("down", 2, "m"), ("near", 6), ("share_down", 1, "m"), ("near", 2), ("near", 3),
    ("across", 7), ("share_down", 2, "p"), ("share", 0), ("up", 2, "p"), ("up", 2, "m"), ("near", 4), ("far", 5), ("share_up", 2, "p"),
    ("share_up", 2, "m"), ("across", 8), ("share_down", 2, "m"), ("conv", 0), ("share", 1), ("down", 3, "p"), ("down", 3, "m"), ("far", 2),
    ("far", 6), ("share", 2), ("conv", 1), ("conv", 2), ("far", 3), ("share", 3), ("share_down", 3, "p"), ("near", 7), ("far", 4),
    ("share", 4), ("conv", 3), ("up", 3, "p"), ("up", 3, "m"), ("near", 8), ("share_up", 3, "p"), ("share_up", 3, "m"), ("conv", 4),
    ("share", 5), ("down", 4, "p"), ("down", 4, "m"), ("share_down", 3, "m"), ("down_far",), ("share", 6), ("far", 7), ("share", 7), ("conv", 5),
    ("up", 4, "p"), ("up", 4, "m"), ("far", 8), ("share", 8), ("share_up", 4), ("conv", 6), ("conv", 7), ("share_down", 4), ("conv", 8),
)


def gelu(v):
    return 0.5 * v * (1.0 + jnp.tanh(0.7978845608028654 * (v + 0.044715 * (v * v * v))))


def nt(a, b):
    return lax.dot_general(a, b, (((1,), (1,)), ((), ())), preferred_element_type=jnp.float32)


class Copies:
    def __init__(self, send_sem, recv_sem):
        self.send_sem, self.recv_sem = send_sem, recv_sem
        self.made, self.arrived = {}, set()

    def send(self, name, src, dst, device):
        i = len(self.made)
        copy = pltpu.make_async_remote_copy(
            src_ref=src, dst_ref=dst, send_sem=self.send_sem.at[i], recv_sem=self.recv_sem.at[i],
            device_id=device, device_id_type=MESH,
        )
        copy.start()
        self.made[name] = copy

    def wait(self, *names):
        for name in names:
            if name not in self.arrived:
                self.arrived.add(name)
                self.made[name].wait_recv()

    def finish(self):
        for name, copy in self.made.items():
            self.wait(name)
            copy.wait_send()


def kernel(
    patches_hbm, embed_hbm, conv_hbm, up_hbm, down_hbm, embed_bias_hbm, conv_bias_hbm, gain_hbm, up_bias_hbm, down_bias_hbm,
    out_ref,
    wc, wu, wd, bu, patches, we, vecs, ub, act, embedded, views, left, right, first, last, total, normed,
    local_sem, send_sem, recv_sem,
):
    lon, lat = lax.axis_index("lon"), lax.axis_index("lat")
    z, y_lo, core = lon // 4, (lon // 2) % 2, lon % 2
    y_hi, x = lat // NX, lat % NX

    def device(x, y_hi, z, y_lo, core):
        return {"lon": z * 4 + y_lo * 2 + core, "lat": y_hi * NX + x}

    def along_x(d):
        return (x + d + NX) % NX

    def along_z(d):
        return (z + d + NZ) % NZ

    right_x, left_x = device(along_x(1), y_hi, z, y_lo, core), device(along_x(-1), y_hi, z, y_lo, core)
    up_z, down_z = device(x, y_hi, along_z(1), y_lo, core), device(x, y_hi, along_z(-1), y_lo, core)
    across_hi = device(x, 1 - y_hi, z, 1 - y_lo, core)
    across_lo = device(x, y_hi, z, 1 - y_lo, core)
    twin = device(x, y_hi, z, y_lo, 1 - core)

    def token(dlat, dlon):
        return {"lon": (lon + dlon + 32) % 32, "lat": (lat + dlat + 8) % 8}

    around = [token(a, b) for a in (-1, 0, 1) for b in (-1, 0, 1) if a or b]

    local = {}

    def fetch(name, src, dst):
        local[name] = pltpu.make_async_copy(src, dst, local_sem.at[len(local)])
        local[name].start()

    fetch("patches", patches_hbm, patches)
    fetch("embed", embed_hbm, we)
    for i, vec in enumerate((embed_bias_hbm, conv_bias_hbm, gain_hbm, down_bias_hbm)):
        fetch(("vec", i), vec, vecs.at[i])
    fetch("up_bias", up_bias_hbm, ub)
    fetch("conv", conv_hbm.at[:, core], wc.at[:, y_hi, x, core])
    fetch("up", up_hbm, wu.at[z, y_lo, core])
    fetch("down", down_hbm, wd.at[z, y_lo, core])

    barrier = pltpu.get_barrier_semaphore()
    partners = [right_x, left_x, up_z, down_z, across_hi, across_lo, twin] + around
    for partner in partners:
        pl.semaphore_signal(barrier, inc=1, device_id=partner, device_id_type=MESH)
    pl.semaphore_wait(barrier, len(partners))

    net = Copies(send_sem, recv_sem)
    taps = wc.reshape(TAPS, WIDTH, WIDTH)
    links = {1: right_x, -1: left_x}
    z_links = {"p": (1, up_z), "m": (-1, down_z)}

    def own(t):
        src, dst = conv_hbm.at[t, core], wc.at[t, y_hi, x, core]
        net.send(("own_hi", t), src, dst, across_hi)
        net.send(("own_x", t, 1), src, dst, right_x)
        net.send(("own_x", t, -1), src, dst, left_x)

    def across(t):
        net.wait(("own_hi", t))
        block = wc.at[t, 1 - y_hi, x, core]
        for d, link in links.items():
            net.send(("other_x", t, d), block, block, link)

    def near(t):
        for d in links:
            net.wait(("own_x", t, d))
            if Y_FIRST[t]:
                net.wait(("other_x", t, d))
        d = WAY[t]
        block = wc.at[t, :, along_x(-d), core] if Y_FIRST[t] else wc.at[t, y_hi, along_x(-d), core]
        net.send(("far", t), block, block, links[d])
        if not Y_FIRST[t]:
            for d in links:
                block = wc.at[t, y_hi, along_x(-d), core]
                net.send(("near_hi", t, d), block, block, across_hi)

    def far(t):
        net.wait(("far", t))
        if not Y_FIRST[t]:
            block = wc.at[t, y_hi, along_x(2), core]
            net.send(("far_hi", t), block, block, across_hi)

    def share(t):
        net.wait(("far", t))
        if not Y_FIRST[t]:
            net.wait(("own_hi", t), ("near_hi", t, 1), ("near_hi", t, -1), ("far_hi", t))
        if "conv" in local:
            local.pop("conv").wait()
        block = wc.at[t, :, :, core]
        net.send(("share", t), block, block, twin)

    def conv(t):
        net.wait(("share", t))
        if "halo" not in local:
            local["halo"] = None
            frame()
        a, b = t // 3, t % 3

        @pl.loop(0, WIDTH // TILE)
        def _(i):
            columns = pl.ds(pl.multiple_of(i * TILE, TILE), TILE)
            weight = taps[t, columns]
            term = nt(views[b, a * COLS : a * COLS + TOKENS], weight)
            if t == 0:
                total[:, columns] = term
            else:
                total[:, columns] += term

    def mlp():
        net.send("up_lo", up_hbm, wu.at[z, y_lo, core], across_lo)
        for s, (_, link) in z_links.items():
            net.send(("up_own", s), up_hbm, wu.at[z, y_lo, core], link)
        for s, (_, link) in z_links.items():
            net.send(("down", 1, s), down_hbm, wd.at[z, y_lo, core], link)
        net.send(("down_lo", 0), down_hbm, wd.at[z, y_lo, core], across_lo)
        local.pop("up_bias").wait()
        bu[z, y_lo, core] = pltpu.roll(ub[...], UNITS * (2 * y_lo + core), 1)
        piece = bu.at[z, y_lo, core]
        net.send("bias_lo", piece, piece, across_lo)
        for s, (_, link) in z_links.items():
            net.send(("bias_own", s), piece, piece, link)

    def mlp_y():
        net.wait("up_lo", "bias_lo")
        block, piece = wu.at[z, 1 - y_lo, core], bu.at[z, 1 - y_lo, core]
        for s, (_, link) in z_links.items():
            net.send(("up_other", s), block, block, link)
            net.send(("bias_other", s), piece, piece, link)

    def wait_up(k, s):
        if k == 1:
            net.wait(("up_own", s), ("up_other", s), ("bias_own", s), ("bias_other", s))
        else:
            net.wait(("up", k, s))
            if k < 4 or s == "p":
                net.wait(("bias", k, s))

    def up(k, s):
        wait_up(k, s)
        if k < 4:
            d, link = z_links[s]
            block, piece = wu.at[along_z(-d * k), :, core], bu.at[along_z(-d * k), :, core]
            if k == 3:
                block = block.at[:, pl.ds(0 if s == "p" else HALF, HALF)]
            net.send(("up", k + 1, s), block, block, link)
            if k < 3 or s == "p":
                net.send(("bias", k + 1, s), piece, piece, link)

    def down(k, s):
        net.wait(("down", k, s))
        if k < 4:
            d, link = z_links[s]
            block = wd.at[along_z(-d * k), y_lo, core]
            part = block if k < 3 else block.at[pl.ds(0 if s == "p" else HALF, HALF)]
            net.send(("down", k + 1, s), part, part, link)
            net.send(("down_lo", k, s), block, block, across_lo)

    def down_far():
        net.wait(("down", 4, "p"), ("down", 4, "m"))
        block = wd.at[along_z(4), y_lo, core]
        net.send(("down_lo", 4), block, block, across_lo)

    def share_up(k, s="p"):
        if k == 0:
            net.wait("up_lo", "bias_lo")
            local.pop("up").wait()
        else:
            wait_up(k, s)
        if k == 4:
            wait_up(k, "m")
        d = z_links[s][0]
        block, piece = wu.at[along_z(-d * k), :, core], bu.at[along_z(-d * k), :, core]
        net.send(("share_up", k, s), block, block, twin)
        net.send(("share_bias", k, s), piece, piece, twin)

    def share_down(k, s="p"):
        if k == 0:
            net.wait(("down_lo", 0))
            local.pop("down").wait()
        elif k == 4:
            net.wait(("down_lo", 4), ("down", 4, "p"), ("down", 4, "m"))
        else:
            net.wait(("down_lo", k, s), ("down", k, s))
        block = wd.at[along_z(-z_links[s][0] * k), :, core]
        net.send(("share_down", k, s), block, block, twin)

    def embed():
        for name in ("patches", "embed", *(("vec", i) for i in range(4))):
            local.pop(name).wait()

        @pl.loop(0, WIDTH // TILE)
        def _(i):
            columns = pl.ds(pl.multiple_of(i * TILE, TILE), TILE)
            value = jnp.dot(patches[...], we[:, columns], preferred_element_type=jnp.float32)
            value = (value + vecs[0, :, columns]).astype(jnp.bfloat16)
            embedded[:, columns] = value
            value = gelu(value.astype(jnp.float32)).astype(jnp.bfloat16)
            views[1, COLS : COLS + TOKENS, columns] = value
            act[:, columns] = value.astype(jnp.float32)

        for i in range(ROWS):
            first[i : i + 1] = act[i * COLS : i * COLS + 1]
            last[i : i + 1] = act[i * COLS + COLS - 1 : i * COLS + COLS]
        net.send("row_after", views.at[1, pl.ds(TOKENS, COLS)], views.at[1, pl.ds(0, COLS)], token(1, 0))
        net.send("row_before", views.at[1, pl.ds(COLS, COLS)], views.at[1, pl.ds(TOKENS + COLS, COLS)], token(-1, 0))
        for a in (0, 1, -1):
            net.send(("col_after", a), last, left.at[1 - a], token(a, 1))
            net.send(("col_before", a), first, right.at[1 - a], token(a, -1))

    def frame():
        net.wait("row_after", "row_before", *((n, a) for n in ("col_after", "col_before") for a in (0, 1, -1)))
        place = lax.broadcasted_iota(jnp.int32, (COLS, WIDTH), 0)
        for i in range(ROWS + 2):
            rows = slice(i * COLS, (i + 1) * COLS)
            slot, row = (0, ROWS - 1) if i == 0 else (2, 0) if i == ROWS + 1 else (1, i - 1)
            if 0 < i <= ROWS:
                middle = act[(i - 1) * COLS : i * COLS]
            else:
                middle = views[1, rows].astype(jnp.float32)
            before = jnp.where(place == 0, left[slot, row : row + 1], pltpu.roll(middle, 1, 0))
            after = jnp.where(place == COLS - 1, right[slot, row : row + 1], pltpu.roll(middle, COLS - 1, 0))
            if i in (0, ROWS + 1):
                inside = lat > 0 if i == 0 else lat < 7
                middle, before, after = (jnp.where(inside, v, 0.0) for v in (middle, before, after))
                views[1, rows] = middle.astype(jnp.bfloat16)
            views[0, rows] = before.astype(jnp.bfloat16)
            views[2, rows] = after.astype(jnp.bfloat16)

    steps = dict(
        own=own, across=across, near=near, far=far, share=share, conv=conv, mlp=mlp, mlp_y=mlp_y, up=up, down=down,
        down_far=down_far, share_up=share_up, share_down=share_down, embed=embed,
    )
    for name, *args in ORDER:
        steps[name](*args)

    for k, s in ((0, "p"), (1, "p"), (1, "m"), (2, "p"), (2, "m"), (3, "p"), (3, "m"), (4, "p")):
        net.wait(("share_up", k, s), ("share_bias", k, s), ("share_down", k, s))

    mixed = (embedded[...].astype(jnp.float32) + total[...] + vecs[1]).astype(jnp.bfloat16).astype(jnp.float32)
    center = jnp.mean(mixed, axis=1, keepdims=True)
    spread = jnp.mean((mixed - center) ** 2, axis=1, keepdims=True)
    normed[...] = ((mixed - center) * lax.rsqrt(spread + 1e-05) * vecs[2]).astype(jnp.bfloat16)
    total[...] = mixed + vecs[3]

    @pl.loop(0, NZ)
    def _(j):
        bias = jnp.sum(bu[j].reshape(4, 8, 4 * UNITS), axis=0)[:1]
        hidden = gelu(nt(normed[...], wu[j].reshape(4 * UNITS, WIDTH)) + bias).astype(jnp.bfloat16)
        total[...] += jnp.dot(hidden, wd[j].reshape(4 * UNITS, WIDTH), preferred_element_type=jnp.float32)

    out_ref[...] = total[...].astype(jnp.bfloat16)
    net.finish()


def body(patches, embed_weight, embed_bias, conv_weight, conv_bias, norm_gain, up_weight, up_bias, down_weight, down_bias):
    rows, cols, inputs = patches.shape
    bf16, f32 = jnp.bfloat16, jnp.float32
    out = pl.pallas_call(
        kernel,
        out_shape=jax.ShapeDtypeStruct((TOKENS, WIDTH), bf16),
        in_specs=[pl.BlockSpec(memory_space=pl.ANY)] * 10,
        out_specs=pl.BlockSpec(memory_space=pltpu.VMEM),
        scratch_shapes=[
            pltpu.VMEM((TAPS, 2, NX, 2, HALF, WIDTH), bf16),
            pltpu.VMEM((NZ, 2, 2, UNITS, WIDTH), bf16),
            pltpu.VMEM((NZ, 2, 2, UNITS, WIDTH), bf16),
            pltpu.VMEM((NZ, 2, 2, 8, 4 * UNITS), f32),
            pltpu.VMEM((TOKENS, inputs), bf16),
            pltpu.VMEM((inputs, WIDTH), bf16),
            pltpu.VMEM((4, 1, WIDTH), f32),
            pltpu.VMEM((8, 4 * UNITS), f32),
            pltpu.VMEM((TOKENS, WIDTH), f32),
            pltpu.VMEM((TOKENS, WIDTH), bf16),
            pltpu.VMEM((3, TOKENS + 2 * COLS, WIDTH), bf16),
            pltpu.VMEM((3, ROWS, WIDTH), f32),
            pltpu.VMEM((3, ROWS, WIDTH), f32),
            pltpu.VMEM((ROWS, WIDTH), f32),
            pltpu.VMEM((ROWS, WIDTH), f32),
            pltpu.VMEM((TOKENS, WIDTH), f32),
            pltpu.VMEM((TOKENS, WIDTH), bf16),
            pltpu.SemaphoreType.DMA((10,)),
            pltpu.SemaphoreType.DMA((160,)),
            pltpu.SemaphoreType.DMA((160,)),
        ],
        compiler_params=pltpu.CompilerParams(collective_id=0, has_side_effects=True, vmem_limit_bytes=56 << 20),
        cost_estimate=pl.CostEstimate(flops=5_570_000_000, bytes_accessed=5_000_000, transcendentals=1_000_000),
        name="block",
    )(
        patches.reshape(TOKENS, inputs),
        embed_weight,
        jnp.swapaxes(conv_weight, 2, 3).reshape(TAPS, 2, HALF, WIDTH),
        up_weight.T,
        down_weight.T,
        embed_bias.reshape(1, WIDTH),
        conv_bias.reshape(1, WIDTH),
        norm_gain.reshape(1, WIDTH),
        jnp.pad(up_bias, ((0, 7), (0, 3 * UNITS))),
        down_bias.reshape(1, WIDTH),
    )
    return out.reshape(rows, cols, WIDTH)


def solution(mesh):
    in_specs = (
        P("lat", "lon", None),
        P(),
        P(),
        P(None, None, None, "lat"),
        P(),
        P(),
        P(None, "lon"),
        P(None, "lon"),
        P(None, "lon"),
        P(),
    )
    return jax.shard_map(body, mesh=mesh, in_specs=in_specs, out_specs=P("lat", "lon", None), check_vma=False)
```

```python
import functools

import jax
import jax.numpy as jnp
from jax import lax
from jax.experimental import pallas as pl
from jax.experimental.pallas import tpu as pltpu
from jax.sharding import PartitionSpec as P

MESH = pl.DeviceIdType.MESH
NX, NZ = 4, 8
ROWS, COLS, WIDTH, UNITS = 8, 32, 768, 96
TOKENS, HALF, TILE = ROWS * COLS, UNITS // 2, 256
TAPS = 9
Y_FIRST = (0, 0, 1, 1, 1, 0, 0, 1, 1)
WAY = (-1, -1, 1, -1, 1, 1, -1, -1, 1)
ORDER = (
    ("own", 0), ("own", 1), ("own", 2), ("own", 3), ("own", 4), ("mlp",), ("embed",), ("near", 0), ("near", 1), ("own", 5),
    ("own", 6), ("mlp_y",), ("across", 2), ("share_up", 0), ("across", 3), ("own", 7), ("share_down", 0), ("across", 4), ("down", 1, "p"),
    ("down", 1, "m"), ("far", 0), ("own", 8), ("up", 1, "p"), ("up", 1, "m"), ("far", 1), ("share_up", 1, "p"), ("share_up", 1, "m"),
    ("share_down", 1, "p"), ("near", 5), ("down", 2, "p"), ("down", 2, "m"), ("near", 6), ("share_down", 1, "m"), ("near", 2), ("near", 3),
    ("across", 7), ("share_down", 2, "p"), ("share", 0), ("up", 2, "p"), ("up", 2, "m"), ("near", 4), ("far", 5), ("share_up", 2, "p"),
    ("share_up", 2, "m"), ("across", 8), ("share_down", 2, "m"), ("conv", 0), ("share", 1), ("down", 3, "p"), ("down", 3, "m"), ("far", 2),
    ("far", 6), ("share", 2), ("conv", 1), ("conv", 2), ("far", 3), ("share", 3), ("share_down", 3, "p"), ("near", 7), ("far", 4),
    ("share", 4), ("conv", 3), ("up", 3, "p"), ("up", 3, "m"), ("near", 8), ("share_up", 3, "p"), ("share_up", 3, "m"), ("conv", 4),
    ("share", 5), ("down", 4, "p"), ("down", 4, "m"), ("share_down", 3, "m"), ("down_far",), ("share", 6), ("far", 7), ("share", 7), ("conv", 5),
    ("up", 4, "p"), ("up", 4, "m"), ("far", 8), ("share", 8), ("share_up", 4), ("conv", 6), ("conv", 7), ("share_down", 4), ("conv", 8),
)


def gelu(v):
    return 0.5 * v * (1.0 + jnp.tanh(0.7978845608028654 * (v + 0.044715 * (v * v * v))))


def nt(a, b):
    return lax.dot_general(a, b, (((1,), (1,)), ((), ())), preferred_element_type=jnp.float32)


class Copies:
    def __init__(self, send_sem, recv_sem):
        self.send_sem, self.recv_sem = send_sem, recv_sem
        self.made, self.arrived = {}, set()

    def send(self, name, src, dst, device):
        i = len(self.made)
        copy = pltpu.make_async_remote_copy(
            src_ref=src, dst_ref=dst, send_sem=self.send_sem.at[i], recv_sem=self.recv_sem.at[i],
            device_id=device, device_id_type=MESH,
        )
        copy.start()
        self.made[name] = copy

    def wait(self, *names):
        for name in names:
            if name not in self.arrived:
                self.arrived.add(name)
                self.made[name].wait_recv()

    def finish(self):
        for name, copy in self.made.items():
            self.wait(name)
            copy.wait_send()


def kernel(
    patches_hbm, embed_hbm, conv_hbm, up_hbm, down_hbm, embed_bias_hbm, conv_bias_hbm, gain_hbm, up_bias_hbm, down_bias_hbm,
    out_ref,
    wc, wu, wd, bu, patches, we, v0, v1, v2, v3, ub, act, embedded, views, left, right, first, last, total, normed, hidden, bias,
    local_sem, send_sem, recv_sem,
):
    vecs = (v0, v1, v2, v3)
    lon, lat = lax.axis_index("lon"), lax.axis_index("lat")
    z, y_lo, core = lon // 4, (lon // 2) % 2, lon % 2
    y_hi, x = lat // NX, lat % NX

    def device(x, y_hi, z, y_lo, core):
        return {"lon": z * 4 + y_lo * 2 + core, "lat": y_hi * NX + x}

    def along_x(d):
        return (x + d + NX) % NX

    def along_z(d):
        return (z + d + NZ) % NZ

    right_x, left_x = device(along_x(1), y_hi, z, y_lo, core), device(along_x(-1), y_hi, z, y_lo, core)
    up_z, down_z = device(x, y_hi, along_z(1), y_lo, core), device(x, y_hi, along_z(-1), y_lo, core)
    across_hi = device(x, 1 - y_hi, z, 1 - y_lo, core)
    across_lo = device(x, y_hi, z, 1 - y_lo, core)
    twin = device(x, y_hi, z, y_lo, 1 - core)

    def token(dlat, dlon):
        return {"lon": (lon + dlon + 32) % 32, "lat": (lat + dlat + 8) % 8}

    around = [token(a, b) for a in (-1, 0, 1) for b in (-1, 0, 1) if a or b]

    local = {}

    def fetch(name, src, dst):
        local[name] = pltpu.make_async_copy(src, dst, local_sem.at[len(local)])
        local[name].start()

    fetch("patches", patches_hbm, patches)
    fetch("embed", embed_hbm, we)
    for i, vec in enumerate((embed_bias_hbm, conv_bias_hbm, gain_hbm, down_bias_hbm)):
        fetch(("vec", i), vec, vecs[i])
    fetch("up_bias", up_bias_hbm, ub)
    fetch("conv", conv_hbm.at[:, core], wc.at[:, y_hi, x, core])
    fetch("up", up_hbm, wu.at[z, y_lo, core])
    fetch("down", down_hbm, wd.at[z, y_lo, core])

    barrier = pltpu.get_barrier_semaphore()
    partners = [right_x, left_x, up_z, down_z, across_hi, across_lo, twin] + around
    for partner in partners:
        pl.semaphore_signal(barrier, inc=1, device_id=partner, device_id_type=MESH)
    pl.semaphore_wait(barrier, len(partners))

    net = Copies(send_sem, recv_sem)
    taps = wc.reshape(TAPS, WIDTH, WIDTH)
    links = {1: right_x, -1: left_x}
    z_links = {"p": (1, up_z), "m": (-1, down_z)}

    def own(t):
        src, dst = conv_hbm.at[t, core], wc.at[t, y_hi, x, core]
        net.send(("own_hi", t), src, dst, across_hi)
        net.send(("own_x", t, 1), src, dst, right_x)
        net.send(("own_x", t, -1), src, dst, left_x)

    def across(t):
        net.wait(("own_hi", t))
        block = wc.at[t, 1 - y_hi, x, core]
        for d, link in links.items():
            net.send(("other_x", t, d), block, block, link)

    def near(t):
        for d in links:
            net.wait(("own_x", t, d))
            if Y_FIRST[t]:
                net.wait(("other_x", t, d))
        d = WAY[t]
        block = wc.at[t, :, along_x(-d), core] if Y_FIRST[t] else wc.at[t, y_hi, along_x(-d), core]
        net.send(("far", t), block, block, links[d])
        if not Y_FIRST[t]:
            for d in links:
                block = wc.at[t, y_hi, along_x(-d), core]
                net.send(("near_hi", t, d), block, block, across_hi)

    def far(t):
        net.wait(("far", t))
        if not Y_FIRST[t]:
            block = wc.at[t, y_hi, along_x(2), core]
            net.send(("far_hi", t), block, block, across_hi)

    def share(t):
        net.wait(("far", t))
        if not Y_FIRST[t]:
            net.wait(("own_hi", t), ("near_hi", t, 1), ("near_hi", t, -1), ("far_hi", t))
        if "conv" in local:
            local.pop("conv").wait()
        block = wc.at[t, :, :, core]
        net.send(("share", t), block, block, twin)

    def conv(t):
        net.wait(("share", t))
        if "halo" not in local:
            local["halo"] = None
            frame()
        a, b = t // 3, t % 3

        term = nt(views[b, a * COLS : a * COLS + TOKENS], taps[t])
        total[...] = term if t == 0 else total[...] + term

    def mlp():
        net.send("up_lo", up_hbm, wu.at[z, y_lo, core], across_lo)
        for s, (_, link) in z_links.items():
            net.send(("up_own", s), up_hbm, wu.at[z, y_lo, core], link)
        for s, (_, link) in z_links.items():
            net.send(("down", 1, s), down_hbm, wd.at[z, y_lo, core], link)
        net.send(("down_lo", 0), down_hbm, wd.at[z, y_lo, core], across_lo)
        local.pop("up_bias").wait()
        spread = jnp.concatenate([ub[...], jnp.zeros((1, 3 * UNITS), jnp.float32)], axis=1)
        spread = jnp.broadcast_to(spread, (8, 4 * UNITS))
        bu[z, y_lo, core] = pltpu.roll(spread, UNITS * (2 * y_lo + core), 1)
        piece = bu.at[z, y_lo, core]
        net.send("bias_lo", piece, piece, across_lo)
        for s, (_, link) in z_links.items():
            net.send(("bias_own", s), piece, piece, link)

    def mlp_y():
        net.wait("up_lo", "bias_lo")
        block, piece = wu.at[z, 1 - y_lo, core], bu.at[z, 1 - y_lo, core]
        for s, (_, link) in z_links.items():
            net.send(("up_other", s), block, block, link)
            net.send(("bias_other", s), piece, piece, link)

    def wait_up(k, s):
        if k == 1:
            net.wait(("up_own", s), ("up_other", s), ("bias_own", s), ("bias_other", s))
        else:
            net.wait(("up", k, s))
            if k < 4 or s == "p":
                net.wait(("bias", k, s))

    def up(k, s):
        wait_up(k, s)
        if k < 4:
            d, link = z_links[s]
            block, piece = wu.at[along_z(-d * k), :, core], bu.at[along_z(-d * k), :, core]
            if k == 3:
                block = block.at[:, pl.ds(0 if s == "p" else HALF, HALF)]
            net.send(("up", k + 1, s), block, block, link)
            if k < 3 or s == "p":
                net.send(("bias", k + 1, s), piece, piece, link)

    def down(k, s):
        net.wait(("down", k, s))
        if k < 4:
            d, link = z_links[s]
            block = wd.at[along_z(-d * k), y_lo, core]
            part = block if k < 3 else block.at[pl.ds(0 if s == "p" else HALF, HALF)]
            net.send(("down", k + 1, s), part, part, link)
            net.send(("down_lo", k, s), block, block, across_lo)

    def down_far():
        net.wait(("down", 4, "p"), ("down", 4, "m"))
        block = wd.at[along_z(4), y_lo, core]
        net.send(("down_lo", 4), block, block, across_lo)

    def share_up(k, s="p"):
        if k == 0:
            net.wait("up_lo", "bias_lo")
            local.pop("up").wait()
        else:
            wait_up(k, s)
        if k == 4:
            wait_up(k, "m")
        d = z_links[s][0]
        block, piece = wu.at[along_z(-d * k), :, core], bu.at[along_z(-d * k), :, core]
        net.send(("share_up", k, s), block, block, twin)
        net.send(("share_bias", k, s), piece, piece, twin)

    def share_down(k, s="p"):
        if k == 0:
            net.wait(("down_lo", 0))
            local.pop("down").wait()
        elif k == 4:
            net.wait(("down_lo", 4), ("down", 4, "p"), ("down", 4, "m"))
        else:
            net.wait(("down_lo", k, s), ("down", k, s))
        block = wd.at[along_z(-z_links[s][0] * k), :, core]
        net.send(("share_down", k, s), block, block, twin)

    def embed():
        for name in ("patches", "embed", *(("vec", i) for i in range(4))):
            local.pop(name).wait()

        value = jnp.dot(patches[...], we[...], preferred_element_type=jnp.float32)
        value = (value + vecs[0][...]).astype(jnp.bfloat16)
        embedded[...] = value
        value = gelu(value.astype(jnp.float32)).astype(jnp.bfloat16)
        views[1, COLS : COLS + TOKENS] = value
        act[...] = value.astype(jnp.float32)
        for i in range(ROWS):
            first[i : i + 1] = act[i * COLS : i * COLS + 1]
            last[i : i + 1] = act[i * COLS + COLS - 1 : i * COLS + COLS]
        net.send("row_after", views.at[1, pl.ds(TOKENS, COLS)], views.at[1, pl.ds(0, COLS)], token(1, 0))
        net.send("row_before", views.at[1, pl.ds(COLS, COLS)], views.at[1, pl.ds(TOKENS + COLS, COLS)], token(-1, 0))
        for a in (0, 1, -1):
            net.send(("col_after", a), last, left.at[1 - a], token(a, 1))
            net.send(("col_before", a), first, right.at[1 - a], token(a, -1))

    def frame():
        net.wait("row_after", "row_before", *((n, a) for n in ("col_after", "col_before") for a in (0, 1, -1)))
        place = lax.broadcasted_iota(jnp.int32, (COLS, WIDTH), 0)
        for i in range(ROWS + 2):
            rows = slice(i * COLS, (i + 1) * COLS)
            slot, row = (0, ROWS - 1) if i == 0 else (2, 0) if i == ROWS + 1 else (1, i - 1)
            if 0 < i <= ROWS:
                middle = act[(i - 1) * COLS : i * COLS]
            else:
                middle = views[1, rows].astype(jnp.float32)
            before = jnp.where(place == 0, left[slot, row : row + 1], pltpu.roll(middle, 1, 0))
            after = jnp.where(place == COLS - 1, right[slot, row : row + 1], pltpu.roll(middle, COLS - 1, 0))
            if i in (0, ROWS + 1):
                inside = lat > 0 if i == 0 else lat < 7
                middle, before, after = (jnp.where(inside, v, 0.0) for v in (middle, before, after))
                views[1, rows] = middle.astype(jnp.bfloat16)
            views[0, rows] = before.astype(jnp.bfloat16)
            views[2, rows] = after.astype(jnp.bfloat16)

    steps = dict(
        own=own, across=across, near=near, far=far, share=share, conv=conv, mlp=mlp, mlp_y=mlp_y, up=up, down=down,
        down_far=down_far, share_up=share_up, share_down=share_down, embed=embed,
    )
    for name, *args in ORDER:
        steps[name](*args)

    for k, s in ((0, "p"), (1, "p"), (1, "m"), (2, "p"), (2, "m"), (3, "p"), (3, "m"), (4, "p")):
        net.wait(("share_up", k, s), ("share_bias", k, s), ("share_down", k, s))

    mixed = (embedded[...].astype(jnp.float32) + total[...] + vecs[1][...]).astype(jnp.bfloat16).astype(jnp.float32)
    center = jnp.mean(mixed, axis=1, keepdims=True)
    spread = jnp.mean((mixed - center) ** 2, axis=1, keepdims=True)
    normed[...] = ((mixed - center) * lax.rsqrt(spread + 1e-05) * vecs[2][...]).astype(jnp.bfloat16)
    total[...] = mixed + vecs[3][...]

    for j in range(NZ):
        units = slice(j * 4 * UNITS, (j + 1) * 4 * UNITS)
        bias[:, units] = jnp.sum(bu[j].reshape(4, 8, 4 * UNITS), axis=0)
    ups, downs = wu.reshape(NZ * 4 * UNITS, WIDTH), wd.reshape(NZ * 4 * UNITS, WIDTH)
    for j in range(NZ * 4 * UNITS // TILE):
        units = slice(j * TILE, (j + 1) * TILE)
        hidden[:, units] = gelu(nt(normed[...], ups[units]) + bias[:1, units]).astype(jnp.bfloat16)
    total[...] += jnp.dot(hidden[...], downs[...], preferred_element_type=jnp.float32)

    out_ref[...] = total[...].astype(jnp.bfloat16)
    net.finish()


def body(patches, embed_weight, embed_bias, conv_weight, conv_bias, norm_gain, up_weight, up_bias, down_weight, down_bias):
    rows, cols, inputs = patches.shape
    bf16, f32 = jnp.bfloat16, jnp.float32
    out = pl.pallas_call(
        kernel,
        out_shape=jax.ShapeDtypeStruct((TOKENS, WIDTH), bf16),
        in_specs=[pl.BlockSpec(memory_space=pl.ANY)] * 10,
        out_specs=pl.BlockSpec(memory_space=pltpu.VMEM),
        scratch_shapes=[
            pltpu.VMEM((TAPS, 2, NX, 2, HALF, WIDTH), bf16),
            pltpu.VMEM((NZ, 2, 2, UNITS, WIDTH), bf16),
            pltpu.VMEM((NZ, 2, 2, UNITS, WIDTH), bf16),
            pltpu.VMEM((NZ, 2, 2, 8, 4 * UNITS), f32),
            pltpu.VMEM((TOKENS, inputs), bf16),
            pltpu.VMEM((inputs, WIDTH), bf16),
            *[pltpu.VMEM((WIDTH,), f32)] * 4,
            pltpu.VMEM((1, UNITS), f32),
            pltpu.VMEM((TOKENS, WIDTH), f32),
            pltpu.VMEM((TOKENS, WIDTH), bf16),
            pltpu.VMEM((3, TOKENS + 2 * COLS, WIDTH), bf16),
            pltpu.VMEM((3, ROWS, WIDTH), f32),
            pltpu.VMEM((3, ROWS, WIDTH), f32),
            pltpu.VMEM((ROWS, WIDTH), f32),
            pltpu.VMEM((ROWS, WIDTH), f32),
            pltpu.VMEM((TOKENS, WIDTH), f32),
            pltpu.VMEM((TOKENS, WIDTH), bf16),
            pltpu.VMEM((TOKENS, NZ * 4 * UNITS), bf16),
            pltpu.VMEM((8, NZ * 4 * UNITS), f32),
            pltpu.SemaphoreType.DMA((10,)),
            pltpu.SemaphoreType.DMA((160,)),
            pltpu.SemaphoreType.DMA((160,)),
        ],
        compiler_params=pltpu.CompilerParams(collective_id=0, has_side_effects=True, vmem_limit_bytes=56 << 20),
        cost_estimate=pl.CostEstimate(flops=5_570_000_000, bytes_accessed=5_000_000, transcendentals=1_000_000),
        name="block",
    )(
        patches.reshape(TOKENS, inputs),
        embed_weight,
        jnp.swapaxes(conv_weight, 2, 3).reshape(TAPS, 2, HALF, WIDTH),
        up_weight.T,
        down_weight.T,
        embed_bias,
        conv_bias,
        norm_gain,
        up_bias,
        down_bias,
    )
    return out.reshape(rows, cols, WIDTH)


def solution(mesh):
    in_specs = (
        P("lat", "lon", None),
        P(),
        P(),
        P(None, None, None, "lat"),
        P(),
        P(),
        P(None, "lon"),
        P(None, "lon"),
        P(None, "lon"),
        P(),
    )
    return jax.shard_map(body, mesh=mesh, in_specs=in_specs, out_specs=P("lat", "lon", None), check_vma=False)
```

```python
import jax
import jax.numpy as jnp
from jax import lax
from jax.experimental import pallas as pl
from jax.experimental.pallas import tpu as pltpu
from jax.sharding import PartitionSpec as P

MESH = pl.DeviceIdType.MESH
NX, NZ = 4, 8
ROWS, COLS, WIDTH, UNITS = 8, 32, 768, 96
TOKENS, HALF, TILE = ROWS * COLS, UNITS // 2, 256
OUT = WIDTH // 2
TAPS = 9
COPIES = 160
WAY = (1, -1, 1, -1, 1, -1, 1, -1, 1)
Y_LINK = {"yd0": "L", "yd4": "L", "yd4m": "L", "ydm": "L", "ydp": "H", "yu0": "L", "yu4": "L", "yum": "H", "yup": "L"}
ORDER = (
    ("mlp",), ("own", 5), ("own", 0), ("embed",), ("own", 1), ("own", 2), ("own", 3), ("own", 4), ("own", 6),
    ("mlp_y",), ("near", 5), ("own", 7), ("up", 1, "p"), ("up", 1, "m"), ("share_up", 0, "p"), ("near", 0),
    ("own", 8), ("halo",), ("near", 1), ("down", 1, "p"), ("down", 1, "m"), ("share_down", 0, "p"), ("near", 2),
    ("other", 1, "p"), ("near", 3), ("other", 1, "m"), ("share_up", 1, "p"), ("near", 4), ("share_down", 1, "m"),
    ("up", 2, "p"), ("up", 2, "m"), ("share_up", 1, "m"), ("near", 6), ("share", 5), ("down", 2, "p"),
    ("down", 2, "m"), ("near", 7), ("frame_other",), ("share", 0), ("conv", 5), ("other", 2, "p"), ("other", 2, "m"),
    ("share_up", 2, "p"), ("near", 8), ("conv", 0), ("share", 1), ("share_down", 1, "p"), ("share", 2), ("conv", 1),
    ("share", 3), ("up", 3, "m"), ("up", 3, "p"), ("share_up", 2, "m"), ("share", 4), ("share_down", 2, "m"),
    ("conv", 2), ("share", 7), ("conv", 3), ("share", 6), ("conv", 4), ("down", 3, "p"), ("down", 3, "m"),
    ("share_down", 2, "p"), ("share", 8), ("conv", 6), ("conv", 7), ("other", 3, "p"), ("other", 3, "m"),
    ("share_up", 3, "p"), ("conv", 8), ("swap",), ("share_up", 3, "m"), ("up", 4, "m"), ("share_down", 3, "p"),
    ("share_down", 3, "m"), ("down", 4, "p"), ("down", 4, "m"), ("share_up", 4, "p"), ("share_down", 4, "p"),
)


def slot(k, s):
    return 7 if k == 4 else 0 if k == 0 else 2 * k - (s == "p")


def gelu(v):
    return 0.5 * v * (1.0 + jnp.tanh(0.7978845608028654 * (v + 0.044715 * (v * v * v))))


def nt(a, b):
    return lax.dot_general(a, b, (((1,), (1,)), ((), ())), preferred_element_type=jnp.float32)


class Copies:
    def __init__(self, send_sem, recv_sem):
        self.send_sem, self.recv_sem = send_sem, recv_sem
        self.made, self.arrived = {}, set()

    def send(self, name, src, dst, device):
        i = len(self.made)
        copy = pltpu.make_async_remote_copy(
            src_ref=src, dst_ref=dst, send_sem=self.send_sem.at[i], recv_sem=self.recv_sem.at[i],
            device_id=device, device_id_type=MESH,
        )
        copy.start()
        self.made[name] = copy

    def wait(self, *names):
        for name in names:
            if name not in self.arrived:
                self.arrived.add(name)
                self.made[name].wait_recv()

    def finish(self):
        for name, copy in self.made.items():
            self.wait(name)
            copy.wait_send()


def kernel(
    patches_hbm, embed_hbm, conv_hbm, up_hbm, down_hbm, embed_bias_hbm, conv_bias_hbm, gain_hbm, up_bias_hbm, down_bias_hbm,
    out_ref,
    wc, wu, wd, bu, patches, we, v0, v1, v2, v3, ub, act, embedded, views, left, right, first, last, edges, total, give, got,
    summed, normed, hidden, bias, local_sem, send_sem, recv_sem,
):
    vecs = (v0, v1, v2, v3)
    lon, lat = lax.axis_index("lon"), lax.axis_index("lat")
    z, y_lo, core = lon // 4, (lon // 2) % 2, lon % 2
    y_hi, x = lat // NX, lat % NX

    def device(x, y_hi, z, y_lo, core):
        return {"lon": z * 4 + y_lo * 2 + core, "lat": y_hi * NX + x}

    def along_x(d):
        return (x + d + NX) % NX

    def along_z(d):
        return (z + d + NZ) % NZ

    x_links = {1: device(along_x(1), y_hi, z, y_lo, core), -1: device(along_x(-1), y_hi, z, y_lo, core)}
    z_links = {"p": device(x, y_hi, along_z(1), y_lo, core), "m": device(x, y_hi, along_z(-1), y_lo, core)}
    pair = device(x, 1 - y_hi, z, 1 - y_lo, core)
    across = device(x, y_hi, z, 1 - y_lo, core)
    y_links = {"L": across, "H": pair}
    twin = device(x, y_hi, z, y_lo, 1 - core)

    def token(dlat, dlon):
        return {"lon": (lon + dlon + 32) % 32, "lat": (lat + dlat + 8) % 8}

    around = [token(a, b) for a in (-1, 0, 1) for b in (-1, 0, 1) if a or b]

    local = {}

    def fetch(name, src, dst):
        local[name] = pltpu.make_async_copy(src, dst, local_sem.at[len(local)])
        local[name].start()

    fetch("patches", patches_hbm, patches)
    fetch("embed", embed_hbm, we)
    for i, vec in enumerate((embed_bias_hbm, conv_bias_hbm, gain_hbm, down_bias_hbm)):
        fetch(("vec", i), vec, vecs[i])
    fetch("up_bias", up_bias_hbm, ub)
    fetch("conv", conv_hbm.at[:, core], wc.at[:, x, core])
    fetch("up", up_hbm, wu.at[0, y_lo, core])
    fetch("down", down_hbm, wd.at[0, y_lo, core])

    barrier = pltpu.get_barrier_semaphore()
    partners = [*x_links.values(), *z_links.values(), pair, across, twin] + around
    for partner in partners:
        pl.semaphore_signal(barrier, inc=1, device_id=partner, device_id_type=MESH)
    pl.semaphore_wait(barrier, len(partners))

    net = Copies(send_sem, recv_sem)
    taps = wc.reshape(TAPS, OUT, WIDTH)

    def own(t):
        for d, link in x_links.items():
            net.send(("own_x", t, d), conv_hbm.at[t, core], wc.at[t, x, core], link)

    def near(t):
        d = WAY[t]
        net.wait(("own_x", t, d))
        block = wc.at[t, along_x(-d), core]
        net.send(("far", t), block, block, x_links[d])

    def share(t):
        net.wait(("own_x", t, 1), ("own_x", t, -1), ("far", t))
        if "conv" in local:
            local.pop("conv").wait()
        block = wc.at[t, :, core]
        net.send(("share", t), block, block, twin)

    def conv(t):
        net.wait(("share", t))
        a, b = t // 3, t % 3
        rows = slice(a * COLS, a * COLS + TOKENS)
        term = nt(jnp.concatenate([views[0, b, rows], views[1, b, rows]]), taps[t])
        total[...] = term if t == 5 else total[...] + term

    def swap():
        give[...] = total[TOKENS:].astype(jnp.bfloat16)
        net.send("swap", give, got, pair)

    def mlp():
        near_half = pl.ds(0, HALF)
        net.send("up_lo", up_hbm.at[near_half], wu.at[0, y_lo, core, near_half], across)
        for s, link in z_links.items():
            net.send(("u", 1, s), up_hbm, wu.at[slot(1, s), y_lo, core], link)
        for s, link in z_links.items():
            net.send(("d", 1, s), down_hbm, wd.at[slot(1, s), y_lo, core], link)
        far_half = pl.ds(HALF, HALF)
        net.send(("yu", 0, "p"), up_hbm.at[far_half], wu.at[0, y_lo, core, far_half], y_links[Y_LINK["yu0"]])
        net.send(("yd", 0, "p"), down_hbm, wd.at[0, y_lo, core], y_links[Y_LINK["yd0"]])
        local.pop("up_bias").wait()
        row = jnp.concatenate([ub[...], jnp.zeros((1, 3 * UNITS), jnp.float32)], axis=1)
        row = jnp.broadcast_to(row, (8, 4 * UNITS))
        bu[0, y_lo, core] = pltpu.roll(row, UNITS * (2 * y_lo + core), 1)
        piece = bu.at[0, y_lo, core]
        net.send("bias_lo", piece, piece, across)
        for s, link in z_links.items():
            net.send(("bias_own", s), piece, bu.at[slot(1, s), y_lo, core], link)

    def mlp_y():
        net.wait("up_lo", "bias_lo")
        half = pl.ds(0, HALF)
        for s, link in z_links.items():
            net.send(("v", 1, s), wu.at[0, 1 - y_lo, core, half], wu.at[slot(1, s), 1 - y_lo, core, half], link)
            net.send(("bias_other", s), bu.at[0, 1 - y_lo, core], bu.at[slot(1, s), 1 - y_lo, core], link)

    def part(k, s):
        return pl.ds(0, UNITS) if k < 3 else pl.ds(0 if s == "p" else HALF, HALF)

    def up(k, s):
        net.wait(("u", k, s))
        here = wu.at[slot(k, s), y_lo, core]
        if k < 4:
            there = wu.at[slot(k + 1, s), y_lo, core]
            net.send(("u", k + 1, s), here.at[part(k, s)], there.at[part(k, s)], z_links[s])
        block = here.at[pl.ds(HALF, HALF)]
        if k < 4:
            net.send(("yu", k, s), block, block, y_links[Y_LINK["yu" + s]])
        else:
            net.send(("yu", k, "p"), block, block, y_links[Y_LINK["yu4"]])

    def down(k, s):
        net.wait(("d", k, s))
        here = wd.at[slot(k, s), y_lo, core]
        if k < 4:
            there = wd.at[slot(k + 1, s), y_lo, core]
            net.send(("d", k + 1, s), here.at[part(k, s)], there.at[part(k, s)], z_links[s])
            net.send(("yd", k, s), here, here, y_links[Y_LINK["yd" + s]])
        else:
            block = here.at[part(3, s)]
            net.send(("yd", k, s), block, block, y_links[Y_LINK["yd4" if s == "p" else "yd4m"]])

    def wait_other(k, s):
        if k == 1:
            net.wait(("v", 1, s), ("bias_own", s), ("bias_other", s))
        elif k < 4:
            net.wait(("v", k, s), ("bias", k, s))
        else:
            net.wait(("v", 4, "p"), ("bias", 4, "m"))

    def other(k, s):
        wait_other(k, s)
        half = pl.ds(0, HALF)
        if k < 3 or s == "p":
            block, there = wu.at[slot(k, s), 1 - y_lo, core, half], wu.at[slot(k + 1, s), 1 - y_lo, core, half]
            net.send(("v", k + 1, s), block, there, z_links[s])
        if k < 3 or s == "m":
            net.send(("bias", k + 1, s), bu.at[slot(k, s), :, core], bu.at[slot(k + 1, s), :, core], z_links[s])

    def share_up(k, s):
        if k == 0:
            net.wait("up_lo", "bias_lo", ("yu", 0, "p"))
            local.pop("up").wait()
        else:
            wait_other(k, s)
            net.wait(("u", k, s), ("yu", k, s))
        if k == 4:
            net.wait(("u", 4, "m"))
        block, piece = wu.at[slot(k, s), :, core], bu.at[slot(k, s), :, core]
        net.send(("share_up", k, s), block, block, twin)
        net.send(("share_bias", k, s), piece, piece, twin)

    def share_down(k, s):
        net.wait(("yd", k, s))
        if k == 0:
            local.pop("down").wait()
        else:
            net.wait(("d", k, s))
        if k == 4:
            net.wait(("d", 4, "m"), ("yd", 4, "m"))
        block = wd.at[slot(k, s), :, core]
        net.send(("share_down", k, s), block, block, twin)

    middle_rows = pl.ds(COLS, TOKENS)

    def embed():
        for name in ("patches", "embed", *(("vec", i) for i in range(4))):
            local.pop(name).wait()
        value = jnp.dot(patches[...], we[...], preferred_element_type=jnp.float32)
        value = (value + vecs[0][...]).astype(jnp.bfloat16)
        embedded[...] = value
        value = gelu(value.astype(jnp.float32)).astype(jnp.bfloat16)
        views[0, 1, COLS : COLS + TOKENS] = value
        act[...] = value.astype(jnp.float32)
        net.send("act", views.at[0, 1, middle_rows], views.at[1, 1, middle_rows], pair)
        for i in range(ROWS):
            first[i : i + 1] = act[i * COLS : i * COLS + 1]
            last[i : i + 1] = act[i * COLS + COLS - 1 : i * COLS + COLS]
        net.send("row_after", views.at[0, 1, pl.ds(TOKENS, COLS)], views.at[0, 1, pl.ds(0, COLS)], token(1, 0))
        net.send("row_before", views.at[0, 1, pl.ds(COLS, COLS)], views.at[0, 1, pl.ds(TOKENS + COLS, COLS)], token(-1, 0))
        for a in (0, 1, -1):
            net.send(("col_after", a), last, left.at[1 - a], token(a, 1))
            net.send(("col_before", a), first, right.at[1 - a], token(a, -1))

    def halo():
        net.wait("row_after", "row_before", *((n, a) for n in ("col_after", "col_before") for a in (0, 1, -1)))
        north, south = lat > 0, lat < 7
        none = jnp.zeros((6, WIDTH), jnp.float32)
        edges[0, :COLS] = jnp.where(north, views[0, 1, :COLS].astype(jnp.float32), 0.0).astype(jnp.bfloat16)
        edges[0, COLS : 2 * COLS] = jnp.where(south, views[0, 1, TOKENS + COLS :].astype(jnp.float32), 0.0).astype(jnp.bfloat16)
        for i, side in enumerate((left, right)):
            above = jnp.where(north, side[0, ROWS - 1 :], 0.0)
            below = jnp.where(south, side[2, :1], 0.0)
            column = jnp.concatenate([above, side[1], below, none], axis=0)
            edges[0, 2 * COLS + 16 * i : 2 * COLS + 16 * (i + 1)] = column.astype(jnp.bfloat16)
        net.send("edge", edges.at[0], edges.at[1], pair)
        frame(0)

    def frame_other():
        net.wait("act", "edge")
        frame(1)

    def frame(own_or_pair):
        place = lax.broadcasted_iota(jnp.int32, (COLS, WIDTH), 0)
        view, edge = views.at[own_or_pair], edges.at[own_or_pair]
        view[1, :COLS] = edge[:COLS]
        view[1, TOKENS + COLS :] = edge[COLS : 2 * COLS]
        columns = edge[2 * COLS :].astype(jnp.float32)
        for i in range(ROWS + 2):
            rows = slice(i * COLS, (i + 1) * COLS)
            middle = view[1, rows].astype(jnp.float32)
            view[0, rows] = jnp.where(place == 0, columns[i : i + 1], pltpu.roll(middle, 1, 0)).astype(jnp.bfloat16)
            after = jnp.where(place == COLS - 1, columns[16 + i : 17 + i], pltpu.roll(middle, COLS - 1, 0))
            view[2, rows] = after.astype(jnp.bfloat16)

    steps = dict(
        own=own, near=near, share=share, conv=conv, swap=swap, mlp=mlp, mlp_y=mlp_y, up=up, down=down, other=other,
        share_up=share_up, share_down=share_down, embed=embed, halo=halo, frame_other=frame_other,
    )
    for name, *args in ORDER:
        steps[name](*args)

    net.wait("swap")
    mine, theirs = total[:TOKENS], got[...].astype(jnp.float32)
    convolved = jnp.concatenate([jnp.where(y_hi == 0, mine, theirs), jnp.where(y_hi == 0, theirs, mine)], axis=1)
    mixed = (embedded[...].astype(jnp.float32) + convolved + vecs[1][...]).astype(jnp.bfloat16).astype(jnp.float32)
    center = jnp.mean(mixed, axis=1, keepdims=True)
    spread = jnp.mean((mixed - center) ** 2, axis=1, keepdims=True)
    normed[...] = ((mixed - center) * lax.rsqrt(spread + 1e-05) * vecs[2][...]).astype(jnp.bfloat16)
    summed[...] = mixed + vecs[3][...]

    def wait_shared(k, s):
        net.wait(("share_up", k, s), ("share_bias", k, s), ("share_down", k, s))
        i = slot(k, s)
        bias[:, i * 4 * UNITS : (i + 1) * 4 * UNITS] = jnp.sum(bu[i].reshape(4, 8, 4 * UNITS), axis=0)

    ups, downs = wu.reshape(NZ * 4 * UNITS, WIDTH), wd.reshape(NZ * 4 * UNITS, WIDTH)

    def hidden_tiles(begin, end):
        for j in range(begin, end):
            units = slice(j * TILE, (j + 1) * TILE)
            hidden[:, units] = gelu(nt(normed[...], ups[units]) + bias[:1, units]).astype(jnp.bfloat16)
        units = slice(begin * TILE, end * TILE)
        return jnp.dot(hidden[:, units], downs[units], preferred_element_type=jnp.float32)

    for k, s in ((0, "p"), (1, "p"), (1, "m"), (2, "p"), (2, "m"), (3, "p"), (3, "m")):
        wait_shared(k, s)
    summed[...] += hidden_tiles(0, 10)
    wait_shared(4, "p")
    out_ref[...] = (summed[...] + hidden_tiles(10, 12)).astype(jnp.bfloat16)
    net.finish()


def body(patches, embed_weight, embed_bias, conv_weight, conv_bias, norm_gain, up_weight, up_bias, down_weight, down_bias):
    rows, cols, inputs = patches.shape
    bf16, f32 = jnp.bfloat16, jnp.float32
    out = pl.pallas_call(
        kernel,
        out_shape=jax.ShapeDtypeStruct((TOKENS, WIDTH), bf16),
        in_specs=[pl.BlockSpec(memory_space=pl.ANY)] * 10,
        out_specs=pl.BlockSpec(memory_space=pltpu.VMEM),
        scratch_shapes=[
            pltpu.VMEM((TAPS, NX, 2, HALF, WIDTH), bf16),
            pltpu.VMEM((NZ, 2, 2, UNITS, WIDTH), bf16),
            pltpu.VMEM((NZ, 2, 2, UNITS, WIDTH), bf16),
            pltpu.VMEM((NZ, 2, 2, 8, 4 * UNITS), f32),
            pltpu.VMEM((TOKENS, inputs), bf16),
            pltpu.VMEM((inputs, WIDTH), bf16),
            *[pltpu.VMEM((WIDTH,), f32)] * 4,
            pltpu.VMEM((1, UNITS), f32),
            pltpu.VMEM((TOKENS, WIDTH), f32),
            pltpu.VMEM((TOKENS, WIDTH), bf16),
            pltpu.VMEM((2, 3, TOKENS + 2 * COLS, WIDTH), bf16),
            pltpu.VMEM((3, ROWS, WIDTH), f32),
            pltpu.VMEM((3, ROWS, WIDTH), f32),
            pltpu.VMEM((ROWS, WIDTH), f32),
            pltpu.VMEM((ROWS, WIDTH), f32),
            pltpu.VMEM((2, 2 * COLS + 32, WIDTH), bf16),
            pltpu.VMEM((2 * TOKENS, OUT), f32),
            pltpu.VMEM((TOKENS, OUT), bf16),
            pltpu.VMEM((TOKENS, OUT), bf16),
            pltpu.VMEM((TOKENS, WIDTH), f32),
            pltpu.VMEM((TOKENS, WIDTH), bf16),
            pltpu.VMEM((TOKENS, NZ * 4 * UNITS), bf16),
            pltpu.VMEM((8, NZ * 4 * UNITS), f32),
            pltpu.SemaphoreType.DMA((10,)),
            pltpu.SemaphoreType.DMA((COPIES,)),
            pltpu.SemaphoreType.DMA((COPIES,)),
        ],
        compiler_params=pltpu.CompilerParams(collective_id=0, has_side_effects=True, vmem_limit_bytes=56 << 20),
        cost_estimate=pl.CostEstimate(flops=5_570_000_000, bytes_accessed=5_000_000, transcendentals=1_000_000),
        name="block",
    )(
        patches.reshape(TOKENS, inputs),
        embed_weight,
        jnp.swapaxes(conv_weight, 2, 3).reshape(TAPS, 2, HALF, WIDTH),
        up_weight.T,
        down_weight.T,
        embed_bias,
        conv_bias,
        norm_gain,
        up_bias,
        down_bias,
    )
    return out.reshape(rows, cols, WIDTH)


def solution(mesh):
    in_specs = (
        P("lat", "lon", None),
        P(),
        P(),
        P(None, None, None, "lat"),
        P(),
        P(),
        P(None, "lon"),
        P(None, "lon"),
        P(None, "lon"),
        P(),
    )
    return jax.shard_map(body, mesh=mesh, in_specs=in_specs, out_specs=P("lat", "lon", None), check_vma=False)
```

```python
import jax
import jax.numpy as jnp
from jax import lax
from jax.experimental import pallas as pl
from jax.experimental.pallas import tpu as pltpu
from jax.sharding import PartitionSpec as P

MESH = pl.DeviceIdType.MESH
NX, NZ = 4, 8
ROWS, COLS, WIDTH, UNITS = 8, 32, 768, 96
TOKENS, HALF, TILE = ROWS * COLS, UNITS // 2, 256
OUT = WIDTH // 2
TAPS = 9
COPIES = 240
PARTS = ("u0", "u1", "d0", "d1")
WAY = (1, -1, 1, -1, 1, -1, 1, -1, 1)
Y_LINK = {"d00": "H", "d04": "L", "d0m": "L", "d0p": "H", "d10": "H", "d14": "L", "d1m": "L", "d1p": "H", "u10": "L", "u14": "L", "u1m": "L", "u1p": "L"}
ORDER = (
    ("own", 0), ("own", 1), ("mlp",), ("embed",), ("own", 2), ("own", 3), ("near", 0), ("mlp_y",),
    ("pass", "u0", 1, "m"), ("pass", "u0", 1, "p"), ("own", 4), ("near", 1), ("share_up", 0, "p"),
    ("pass", "u1", 1, "p"), ("pass", "u1", 1, "m"), ("bias_sum",), ("share_down", 0, "p"), ("halo",), ("own", 5),
    ("pass", "d0", 1, "p"), ("pass", "d0", 1, "m"), ("near", 2), ("own", 6), ("near", 3), ("pass", "d1", 1, "p"),
    ("pass", "d1", 1, "m"), ("own", 7), ("other", 1, "p"), ("other", 1, "m"), ("share_up", 1, "p"),
    ("share_up", 1, "m"), ("share", 0), ("own", 8), ("share", 1), ("pass", "u0", 2, "p"), ("pass", "u0", 2, "m"),
    ("near", 4), ("near", 5), ("pass", "u1", 2, "p"), ("pass", "u1", 2, "m"), ("bias", 1, "p"), ("bias", 1, "m"),
    ("share_down", 1, "m"), ("pass", "d0", 2, "p"), ("pass", "d0", 2, "m"), ("share", 2), ("share", 3),
    ("pass", "d1", 2, "p"), ("pass", "d1", 2, "m"), ("near", 6), ("frame_other",), ("conv", 0), ("other", 2, "m"),
    ("near", 7), ("other", 2, "p"), ("share_up", 2, "p"), ("share_up", 2, "m"), ("conv", 1), ("conv", 2), ("conv", 3),
    ("pass", "u0", 3, "p"), ("near", 8), ("share_down", 1, "p"), ("share", 5), ("share_down", 2, "m"),
    ("pass", "u1", 3, "p"), ("pass", "u1", 3, "m"), ("bias", 2, "p"), ("bias", 2, "m"), ("share", 4), ("conv", 5),
    ("share", 7), ("pass", "d0", 3, "p"), ("pass", "d0", 3, "m"), ("conv", 4), ("share", 6), ("share_down", 2, "p"),
    ("conv", 7), ("pass", "d1", 3, "p"), ("pass", "d1", 3, "m"), ("share", 8), ("conv", 6), ("other", 3, "p"),
    ("share_up", 3, "p"), ("share_up", 3, "m"), ("conv", 8), ("swap",), ("pass", "u1", 4, "m"), ("bias", 3, "m"),
    ("share_down", 3, "p"), ("share_down", 3, "m"), ("pass", "d0", 4, "p"), ("pass", "d1", 4, "m"),
    ("share_up", 4, "p"), ("share_down", 4, "p"),
)


def slot(k, s):
    return 7 if k == 4 else 0 if k == 0 else 2 * k - (s == "p")


def gelu(v):
    return 0.5 * v * (1.0 + jnp.tanh(0.7978845608028654 * (v + 0.044715 * (v * v * v))))


def nt(a, b):
    return lax.dot_general(a, b, (((1,), (1,)), ((), ())), preferred_element_type=jnp.float32)


class Copies:
    def __init__(self, send_sem, recv_sem):
        self.send_sem, self.recv_sem = send_sem, recv_sem
        self.made, self.arrived = {}, set()

    def send(self, name, src, dst, device):
        i = len(self.made)
        copy = pltpu.make_async_remote_copy(
            src_ref=src, dst_ref=dst, send_sem=self.send_sem.at[i], recv_sem=self.recv_sem.at[i],
            device_id=device, device_id_type=MESH,
        )
        copy.start()
        self.made[name] = copy

    def wait(self, *names):
        for name in names:
            if name not in self.arrived:
                self.arrived.add(name)
                self.made[name].wait_recv()

    def finish(self):
        for name, copy in self.made.items():
            self.wait(name)
            copy.wait_send()


def kernel(
    patches_hbm, embed_hbm, conv_hbm, up_hbm, down_hbm, embed_bias_hbm, conv_bias_hbm, gain_hbm, up_bias_hbm, down_bias_hbm,
    out_ref,
    wc, wu, wd, pieces, bias, patches, we, v0, v1, v2, v3, ub, act, embedded, views, left, right, first, last, edges, total, give, got,
    summed, normed, hidden, biases, local_sem, send_sem, recv_sem,
):
    vecs = (v0, v1, v2, v3)
    lon, lat = lax.axis_index("lon"), lax.axis_index("lat")
    z, y_lo, core = lon // 4, (lon // 2) % 2, lon % 2
    y_hi, x = lat // NX, lat % NX

    def device(x, y_hi, z, y_lo, core):
        return {"lon": z * 4 + y_lo * 2 + core, "lat": y_hi * NX + x}

    def along_x(d):
        return (x + d + NX) % NX

    def along_z(d):
        return (z + d + NZ) % NZ

    x_links = {1: device(along_x(1), y_hi, z, y_lo, core), -1: device(along_x(-1), y_hi, z, y_lo, core)}
    z_links = {"p": device(x, y_hi, along_z(1), y_lo, core), "m": device(x, y_hi, along_z(-1), y_lo, core)}
    pair = device(x, 1 - y_hi, z, 1 - y_lo, core)
    across = device(x, y_hi, z, 1 - y_lo, core)
    across_twin = device(x, y_hi, z, 1 - y_lo, 1 - core)
    y_links = {"L": across, "H": pair}
    twin = device(x, y_hi, z, y_lo, 1 - core)

    def token(dlat, dlon):
        return {"lon": (lon + dlon + 32) % 32, "lat": (lat + dlat + 8) % 8}

    around = [token(a, b) for a in (-1, 0, 1) for b in (-1, 0, 1) if a or b]

    local = {}

    def fetch(name, src, dst):
        local[name] = pltpu.make_async_copy(src, dst, local_sem.at[len(local)])
        local[name].start()

    fetch("patches", patches_hbm, patches)
    fetch("embed", embed_hbm, we)
    for i, vec in enumerate((embed_bias_hbm, conv_bias_hbm, gain_hbm, down_bias_hbm)):
        fetch(("vec", i), vec, vecs[i])
    fetch("up_bias", up_bias_hbm, ub)
    fetch("conv", conv_hbm.at[:, core], wc.at[:, x, core])
    fetch("up", up_hbm, wu.at[0, y_lo, core])
    fetch("down", down_hbm, wd.at[0, y_lo, core])

    barrier = pltpu.get_barrier_semaphore()
    partners = [*x_links.values(), *z_links.values(), pair, across, twin, across_twin] + around
    for partner in partners:
        pl.semaphore_signal(barrier, inc=1, device_id=partner, device_id_type=MESH)
    pl.semaphore_wait(barrier, len(partners))

    net = Copies(send_sem, recv_sem)
    taps = wc.reshape(TAPS, OUT, WIDTH)

    def own(t):
        for d, link in x_links.items():
            net.send(("own_x", t, d), conv_hbm.at[t, core], wc.at[t, x, core], link)

    def near(t):
        d = WAY[t]
        net.wait(("own_x", t, d))
        block = wc.at[t, along_x(-d), core]
        net.send(("far", t), block, block, x_links[d])

    def share(t):
        net.wait(("own_x", t, 1), ("own_x", t, -1), ("far", t))
        if "conv" in local:
            local.pop("conv").wait()
        block = wc.at[t, :, core]
        net.send(("share", t), block, block, twin)

    def conv(t):
        net.wait(("share", t))
        a, b = t // 3, t % 3
        rows = slice(a * COLS, a * COLS + TOKENS)
        term = nt(jnp.concatenate([views[0, b, rows], views[1, b, rows]]), taps[t])
        total[...] = term if t == 0 else total[...] + term

    def swap():
        give[...] = total[TOKENS:].astype(jnp.bfloat16)
        net.send("swap", give, got, pair)

    halves = {"0": pl.ds(0, HALF), "1": pl.ds(HALF, HALF)}
    held = {"u": wu, "d": wd}

    def block(p, k, s, lo):
        return held[p[0]].at[slot(k, s), lo, core, halves[p[1]]]

    def mlp():
        given = {"u": up_hbm, "d": down_hbm}
        net.send("up_lo", up_hbm.at[halves["0"]], block("u0", 0, "p", y_lo), across)
        for p in PARTS:
            for s, link in z_links.items():
                net.send((p, 1, s), given[p[0]].at[halves[p[1]]], block(p, 1, s, y_lo), link)
        for p in PARTS[1:]:
            net.send(("y" + p, 0, "p"), given[p[0]].at[halves[p[1]]], block(p, 0, "p", y_lo), y_links[Y_LINK[p + "0"]])
        local.pop("up_bias").wait()
        row = jnp.concatenate([ub[...], jnp.zeros((1, 3 * UNITS), jnp.float32)], axis=1)
        row = pltpu.roll(jnp.broadcast_to(row, (8, 4 * UNITS)), UNITS * (2 * y_lo + core), 1)
        pieces[0] = row[:1]
        for i, chip in enumerate((twin, across, across_twin)):
            net.send(("piece", i), pieces.at[0], pieces.at[i + 1], chip)

    def bias_sum():
        net.wait(*(("piece", i) for i in range(3)))
        bias[0] = pieces[0] + pieces[1] + pieces[2] + pieces[3]
        for s, link in z_links.items():
            net.send(("bias", 1, s), bias.at[0], bias.at[slot(1, s)], link)

    def pass_bias(k, s):
        net.wait(("bias", k, s))
        net.send(("bias", k + 1, s), bias.at[slot(k, s)], bias.at[slot(k + 1, s)], z_links[s])

    def mlp_y():
        net.wait("up_lo")
        for s, link in z_links.items():
            net.send(("v", 1, s), block("u0", 0, s, 1 - y_lo), block("u0", 1, s, 1 - y_lo), link)

    def other(k, s):
        net.wait(("v", k, s))
        net.send(("v", k + 1, s), block("u0", k, s, 1 - y_lo), block("u0", k + 1, s, 1 - y_lo), z_links[s])

    def pass_on(p, k, s):
        net.wait((p, k, s))
        here = block(p, k, s, y_lo)
        if k < 3 or (k == 3 and (p[1] == "0") == (s == "p")):
            net.send((p, k + 1, s), here, block(p, k + 1, s, y_lo), z_links[s])
        if p != "u0":
            net.send(("y" + p, k, s), here, here, y_links[Y_LINK[p + (s if k < 4 else "4")]])

    def share_up(k, s):
        if k == 0:
            net.wait("up_lo", ("yu1", 0, "p"))
            local.pop("up").wait()
        elif k == 4:
            net.wait(("u0", 4, "p"), ("u1", 4, "m"), ("v", 4, "p"), ("yu1", 4, "m"))
        else:
            net.wait(("u0", k, s), ("u1", k, s), ("v", k, s), ("yu1", k, s))
        all_of_core = wu.at[slot(k, s), :, core]
        net.send(("share_up", k, s), all_of_core, all_of_core, twin)

    def share_down(k, s):
        if k == 0:
            net.wait(("yd0", 0, "p"), ("yd1", 0, "p"))
            local.pop("down").wait()
        elif k == 4:
            net.wait(("d0", 4, "p"), ("d1", 4, "m"), ("yd0", 4, "p"), ("yd1", 4, "m"))
        else:
            net.wait(("d0", k, s), ("d1", k, s), ("yd0", k, s), ("yd1", k, s))
        all_of_core = wd.at[slot(k, s), :, core]
        net.send(("share_down", k, s), all_of_core, all_of_core, twin)

    middle_rows = pl.ds(COLS, TOKENS)

    def embed():
        for name in ("patches", "embed", *(("vec", i) for i in range(4))):
            local.pop(name).wait()
        value = jnp.dot(patches[...], we[...], preferred_element_type=jnp.float32)
        value = (value + vecs[0][...]).astype(jnp.bfloat16)
        embedded[...] = value
        value = gelu(value.astype(jnp.float32)).astype(jnp.bfloat16)
        views[0, 1, COLS : COLS + TOKENS] = value
        act[...] = value.astype(jnp.float32)
        net.send("act", views.at[0, 1, middle_rows], views.at[1, 1, middle_rows], pair)
        for i in range(ROWS):
            first[i : i + 1] = act[i * COLS : i * COLS + 1]
            last[i : i + 1] = act[i * COLS + COLS - 1 : i * COLS + COLS]
        net.send("row_after", views.at[0, 1, pl.ds(TOKENS, COLS)], views.at[0, 1, pl.ds(0, COLS)], token(1, 0))
        net.send("row_before", views.at[0, 1, pl.ds(COLS, COLS)], views.at[0, 1, pl.ds(TOKENS + COLS, COLS)], token(-1, 0))
        for a in (0, 1, -1):
            net.send(("col_after", a), last, left.at[1 - a], token(a, 1))
            net.send(("col_before", a), first, right.at[1 - a], token(a, -1))

    def halo():
        net.wait("row_after", "row_before", *((n, a) for n in ("col_after", "col_before") for a in (0, 1, -1)))
        north, south = lat > 0, lat < 7
        none = jnp.zeros((6, WIDTH), jnp.float32)
        edges[0, :COLS] = jnp.where(north, views[0, 1, :COLS].astype(jnp.float32), 0.0).astype(jnp.bfloat16)
        edges[0, COLS : 2 * COLS] = jnp.where(south, views[0, 1, TOKENS + COLS :].astype(jnp.float32), 0.0).astype(jnp.bfloat16)
        for i, side in enumerate((left, right)):
            above = jnp.where(north, side[0, ROWS - 1 :], 0.0)
            below = jnp.where(south, side[2, :1], 0.0)
            column = jnp.concatenate([above, side[1], below, none], axis=0)
            edges[0, 2 * COLS + 16 * i : 2 * COLS + 16 * (i + 1)] = column.astype(jnp.bfloat16)
        net.send("edge", edges.at[0], edges.at[1], pair)
        frame(0)

    def frame_other():
        net.wait("act", "edge")
        frame(1)

    def frame(own_or_pair):
        place = lax.broadcasted_iota(jnp.int32, (COLS, WIDTH), 0)
        view, edge = views.at[own_or_pair], edges.at[own_or_pair]
        view[1, :COLS] = edge[:COLS]
        view[1, TOKENS + COLS :] = edge[COLS : 2 * COLS]
        columns = edge[2 * COLS :].astype(jnp.float32)
        for i in range(ROWS + 2):
            rows = slice(i * COLS, (i + 1) * COLS)
            middle = view[1, rows].astype(jnp.float32)
            view[0, rows] = jnp.where(place == 0, columns[i : i + 1], pltpu.roll(middle, 1, 0)).astype(jnp.bfloat16)
            after = jnp.where(place == COLS - 1, columns[16 + i : 17 + i], pltpu.roll(middle, COLS - 1, 0))
            view[2, rows] = after.astype(jnp.bfloat16)

    steps = dict(
        own=own, near=near, share=share, conv=conv, swap=swap, mlp=mlp, mlp_y=mlp_y, **{"pass": pass_on}, other=other,
        share_up=share_up, share_down=share_down, bias=pass_bias, bias_sum=bias_sum, embed=embed, halo=halo, frame_other=frame_other,
    )
    for name, *args in ORDER:
        steps[name](*args)

    net.wait("swap")
    mine, theirs = total[:TOKENS], got[...].astype(jnp.float32)
    convolved = jnp.concatenate([jnp.where(y_hi == 0, mine, theirs), jnp.where(y_hi == 0, theirs, mine)], axis=1)
    mixed = (embedded[...].astype(jnp.float32) + convolved + vecs[1][...]).astype(jnp.bfloat16).astype(jnp.float32)
    center = jnp.mean(mixed, axis=1, keepdims=True)
    spread = jnp.mean((mixed - center) ** 2, axis=1, keepdims=True)
    normed[...] = ((mixed - center) * lax.rsqrt(spread + 1e-05) * vecs[2][...]).astype(jnp.bfloat16)
    summed[...] = mixed + vecs[3][...]

    def wait_shared(k, s):
        net.wait(("share_up", k, s), ("share_down", k, s), *([("bias", k, "m" if k == 4 else s)] if k else []))
        i = slot(k, s)
        biases[:, i * 4 * UNITS : (i + 1) * 4 * UNITS] = bias[i]

    ups, downs = wu.reshape(NZ * 4 * UNITS, WIDTH), wd.reshape(NZ * 4 * UNITS, WIDTH)

    def hidden_tiles(begin, end):
        for j in range(begin, end):
            units = slice(j * TILE, (j + 1) * TILE)
            hidden[:, units] = gelu(nt(normed[...], ups[units]) + biases[:, units]).astype(jnp.bfloat16)
        units = slice(begin * TILE, end * TILE)
        return jnp.dot(hidden[:, units], downs[units], preferred_element_type=jnp.float32)

    for k, s in ((0, "p"), (1, "p"), (1, "m"), (2, "p"), (2, "m"), (3, "p"), (3, "m")):
        wait_shared(k, s)
    summed[...] += hidden_tiles(0, 10)
    wait_shared(4, "p")
    out_ref[...] = (summed[...] + hidden_tiles(10, 12)).astype(jnp.bfloat16)
    net.finish()


def body(patches, embed_weight, embed_bias, conv_weight, conv_bias, norm_gain, up_weight, up_bias, down_weight, down_bias):
    rows, cols, inputs = patches.shape
    bf16, f32 = jnp.bfloat16, jnp.float32
    out = pl.pallas_call(
        kernel,
        out_shape=jax.ShapeDtypeStruct((TOKENS, WIDTH), bf16),
        in_specs=[pl.BlockSpec(memory_space=pl.ANY)] * 10,
        out_specs=pl.BlockSpec(memory_space=pltpu.VMEM),
        scratch_shapes=[
            pltpu.VMEM((TAPS, NX, 2, HALF, WIDTH), bf16),
            pltpu.VMEM((NZ, 2, 2, UNITS, WIDTH), bf16),
            pltpu.VMEM((NZ, 2, 2, UNITS, WIDTH), bf16),
            pltpu.VMEM((4, 1, 4 * UNITS), f32),
            pltpu.VMEM((NZ, 1, 4 * UNITS), f32),
            pltpu.VMEM((TOKENS, inputs), bf16),
            pltpu.VMEM((inputs, WIDTH), bf16),
            *[pltpu.VMEM((WIDTH,), f32)] * 4,
            pltpu.VMEM((1, UNITS), f32),
            pltpu.VMEM((TOKENS, WIDTH), f32),
            pltpu.VMEM((TOKENS, WIDTH), bf16),
            pltpu.VMEM((2, 3, TOKENS + 2 * COLS, WIDTH), bf16),
            pltpu.VMEM((3, ROWS, WIDTH), f32),
            pltpu.VMEM((3, ROWS, WIDTH), f32),
            pltpu.VMEM((ROWS, WIDTH), f32),
            pltpu.VMEM((ROWS, WIDTH), f32),
            pltpu.VMEM((2, 2 * COLS + 32, WIDTH), bf16),
            pltpu.VMEM((2 * TOKENS, OUT), f32),
            pltpu.VMEM((TOKENS, OUT), bf16),
            pltpu.VMEM((TOKENS, OUT), bf16),
            pltpu.VMEM((TOKENS, WIDTH), f32),
            pltpu.VMEM((TOKENS, WIDTH), bf16),
            pltpu.VMEM((TOKENS, NZ * 4 * UNITS), bf16),
            pltpu.VMEM((1, NZ * 4 * UNITS), f32),
            pltpu.SemaphoreType.DMA((10,)),
            pltpu.SemaphoreType.DMA((COPIES,)),
            pltpu.SemaphoreType.DMA((COPIES,)),
        ],
        compiler_params=pltpu.CompilerParams(collective_id=0, has_side_effects=True, vmem_limit_bytes=56 << 20),
        cost_estimate=pl.CostEstimate(flops=5_570_000_000, bytes_accessed=5_000_000, transcendentals=1_000_000),
        name="block",
    )(
        patches.reshape(TOKENS, inputs),
        embed_weight,
        jnp.swapaxes(conv_weight, 2, 3).reshape(TAPS, 2, HALF, WIDTH),
        up_weight.T,
        down_weight.T,
        embed_bias,
        conv_bias,
        norm_gain,
        up_bias,
        down_bias,
    )
    return out.reshape(rows, cols, WIDTH)


def solution(mesh):
    in_specs = (
        P("lat", "lon", None),
        P(),
        P(),
        P(None, None, None, "lat"),
        P(),
        P(),
        P(None, "lon"),
        P(None, "lon"),
        P(None, "lon"),
        P(),
    )
    return jax.shard_map(body, mesh=mesh, in_specs=in_specs, out_specs=P("lat", "lon", None), check_vma=False)
```

```python
import jax
import jax.numpy as jnp
from jax import lax
from jax.experimental import pallas as pl
from jax.experimental.pallas import tpu as pltpu
from jax.sharding import PartitionSpec as P

MESH = pl.DeviceIdType.MESH
NX, NZ = 4, 8
ROWS, COLS, WIDTH, UNITS = 8, 32, 768, 96
TOKENS, HALF, TILE = ROWS * COLS, UNITS // 2, 256
OUT = WIDTH // 2
TAPS = 9
COPIES = 133
PARTS = range(4)
OWN, NEAR, SHARE, CONV, SWAP, MLP, MLP_Y, PASS, OTHER, SHARE_UP, SHARE_DOWN, EMBED, HALO, FRAME, BIAS, BIAS_SUM = range(16)
WAY = (1, -1, 1, -1, 1, -1, 1, -1, 1)
Y_LINK = {(2, 0): 1, (2, 4): 0, (2, -1): 0, (2, 1): 1, (3, 0): 1, (3, 4): 0, (3, -1): 0, (3, 1): 1, (1, 0): 0, (1, 4): 0, (1, -1): 0, (1, 1): 0}
ORDER = (
    (OWN, 0), (OWN, 1), (MLP,), (EMBED,), (OWN, 2), (OWN, 3), (NEAR, 0), (MLP_Y,), (PASS, 0, 1, -1), (PASS, 0, 1, 1),
    (OWN, 4), (NEAR, 1), (SHARE_UP, 0, 1), (PASS, 1, 1, 1), (PASS, 1, 1, -1), (BIAS_SUM,), (SHARE_DOWN, 0, 1),
    (HALO,), (OWN, 5), (PASS, 2, 1, 1), (PASS, 2, 1, -1), (NEAR, 2), (OWN, 6), (NEAR, 3), (PASS, 3, 1, 1),
    (PASS, 3, 1, -1), (OWN, 7), (OTHER, 1, 1), (OTHER, 1, -1), (SHARE_UP, 1, 1), (SHARE_UP, 1, -1), (SHARE, 0),
    (OWN, 8), (SHARE, 1), (PASS, 0, 2, 1), (PASS, 0, 2, -1), (NEAR, 4), (NEAR, 5), (PASS, 1, 2, 1), (PASS, 1, 2, -1),
    (BIAS, 1, 1), (BIAS, 1, -1), (SHARE_DOWN, 1, -1), (PASS, 2, 2, 1), (PASS, 2, 2, -1), (SHARE, 2), (SHARE, 3),
    (PASS, 3, 2, 1), (PASS, 3, 2, -1), (NEAR, 6), (FRAME,), (CONV, 0), (OTHER, 2, -1), (NEAR, 7), (OTHER, 2, 1),
    (SHARE_UP, 2, 1), (SHARE_UP, 2, -1), (CONV, 1), (CONV, 2), (CONV, 3), (PASS, 0, 3, 1), (NEAR, 8),
    (SHARE_DOWN, 1, 1), (SHARE, 5), (SHARE_DOWN, 2, -1), (PASS, 1, 3, 1), (PASS, 1, 3, -1), (BIAS, 2, 1),
    (BIAS, 2, -1), (SHARE, 4), (CONV, 5), (SHARE, 7), (PASS, 2, 3, 1), (PASS, 2, 3, -1), (CONV, 4), (SHARE, 6),
    (SHARE_DOWN, 2, 1), (CONV, 7), (PASS, 3, 3, 1), (PASS, 3, 3, -1), (SHARE, 8), (CONV, 6), (OTHER, 3, 1),
    (SHARE_UP, 3, 1), (SHARE_UP, 3, -1), (CONV, 8), (SWAP,), (PASS, 1, 4, -1), (BIAS, 3, -1), (SHARE_DOWN, 3, 1),
    (SHARE_DOWN, 3, -1), (PASS, 2, 4, 1), (PASS, 3, 4, -1), (SHARE_UP, 4, 1), (SHARE_DOWN, 4, 1),
)


def slot(k, s):
    return 7 if k == 4 else 0 if k == 0 else 2 * k - (s == 1)


def gelu(v):
    return 0.5 * v * (1.0 + jnp.tanh(0.7978845608028654 * (v + 0.044715 * (v * v * v))))


def nt(a, b):
    return lax.dot_general(a, b, (((1,), (1,)), ((), ())), preferred_element_type=jnp.float32)


class Copies:
    def __init__(self, send_sem, recv_sem):
        self.send_sem, self.recv_sem = send_sem, recv_sem
        self.made, self.arrived = {}, set()

    def send(self, name, src, dst, device):
        i = len(self.made)
        copy = pltpu.make_async_remote_copy(
            src_ref=src, dst_ref=dst, send_sem=self.send_sem.at[0], recv_sem=self.recv_sem.at[i],
            device_id=device, device_id_type=MESH,
        )
        copy.start()
        self.made[name] = copy

    def wait(self, *names):
        for name in names:
            if name not in self.arrived:
                self.arrived.add(name)
                self.made[name].wait_recv()

    def finish(self):
        for name, copy in self.made.items():
            self.wait(name)
        for copy in self.made.values():
            copy.wait_send()


def kernel(
    patches_hbm, embed_hbm, conv_hbm, up_hbm, down_hbm, embed_bias_hbm, conv_bias_hbm, gain_hbm, up_bias_hbm, down_bias_hbm,
    out_ref,
    wc, wu, wd, pieces, bias, patches, we, v0, v1, v2, v3, ub, act, embedded, views, left, right, first, last, edges, total, give, got,
    summed, normed, hidden, biases, local_sem, send_sem, recv_sem,
):
    vecs = (v0, v1, v2, v3)
    lon, lat = lax.axis_index("lon"), lax.axis_index("lat")
    z, y_lo, core = lon // 4, (lon // 2) % 2, lon % 2
    y_hi, x = lat // NX, lat % NX

    def device(x, y_hi, z, y_lo, core):
        return {"lon": z * 4 + y_lo * 2 + core, "lat": y_hi * NX + x}

    def along_x(d):
        return (x + d + NX) % NX

    def along_z(d):
        return (z + d + NZ) % NZ

    x_links = {1: device(along_x(1), y_hi, z, y_lo, core), -1: device(along_x(-1), y_hi, z, y_lo, core)}
    z_links = {1: device(x, y_hi, along_z(1), y_lo, core), -1: device(x, y_hi, along_z(-1), y_lo, core)}
    pair = device(x, 1 - y_hi, z, 1 - y_lo, core)
    across = device(x, y_hi, z, 1 - y_lo, core)
    across_twin = device(x, y_hi, z, 1 - y_lo, 1 - core)
    y_links = (across, pair)
    twin = device(x, y_hi, z, y_lo, 1 - core)

    def token(dlat, dlon):
        return {"lon": (lon + dlon + 32) % 32, "lat": (lat + dlat + 8) % 8}

    around = [token(a, b) for a in (-1, 0, 1) for b in (-1, 0, 1) if a or b]

    local = {}

    def fetch(name, src, dst):
        local[name] = pltpu.make_async_copy(src, dst, local_sem.at[len(local)])
        local[name].start()

    fetch("patches", patches_hbm, patches)
    fetch("embed", embed_hbm, we)
    for i, vec in enumerate((embed_bias_hbm, conv_bias_hbm, gain_hbm, down_bias_hbm)):
        fetch(("vec", i), vec, vecs[i])
    fetch("up_bias", up_bias_hbm, ub)
    fetch("conv", conv_hbm.at[:, core], wc.at[:, x, core])
    fetch("up", up_hbm, wu.at[0, y_lo, core])
    fetch("down", down_hbm, wd.at[0, y_lo, core])

    barrier = pltpu.get_barrier_semaphore()
    partners = [*x_links.values(), *z_links.values(), pair, across, twin, across_twin] + around
    for partner in partners:
        pl.semaphore_signal(barrier, inc=1, device_id=partner, device_id_type=MESH)
    pl.semaphore_wait(barrier, len(partners))

    net = Copies(send_sem, recv_sem)
    taps = wc.reshape(TAPS, OUT, WIDTH)

    def own(t):
        for d, link in x_links.items():
            net.send(("own_x", t, d), conv_hbm.at[t, core], wc.at[t, x, core], link)

    def near(t):
        d = WAY[t]
        net.wait(("own_x", t, d))
        block = wc.at[t, along_x(-d), core]
        net.send(("far", t), block, block, x_links[d])

    def share(t):
        net.wait(("own_x", t, 1), ("own_x", t, -1), ("far", t))
        if "conv" in local:
            local.pop("conv").wait()
        block = wc.at[t, :, core]
        net.send(("share", t), block, block, twin)

    def conv(t):
        net.wait(("share", t))
        a, b = t // 3, t % 3
        rows = slice(a * COLS, a * COLS + TOKENS)
        term = nt(jnp.concatenate([views[0, b, rows], views[1, b, rows]]), taps[t])
        total[...] = term if t == 0 else total[...] + term

    def swap():
        give[...] = total[TOKENS:].astype(jnp.bfloat16)
        net.send("swap", give, got, pair)

    def half(array, p):
        return array.at[pl.ds(p % 2 * HALF, HALF)]

    def block(p, k, s, lo):
        return half((wu if p < 2 else wd).at[slot(k, s), lo, core], p)

    def mlp():
        given = (up_hbm, up_hbm, down_hbm, down_hbm)
        net.send("up_lo", half(up_hbm, 0), block(0, 0, 1, y_lo), across)
        for p in PARTS:
            for s, link in z_links.items():
                net.send((p, 1, s), half(given[p], p), block(p, 1, s, y_lo), link)
        for p in PARTS[1:]:
            net.send(("y", p, 0, 1), half(given[p], p), block(p, 0, 1, y_lo), y_links[Y_LINK[p, 0]])
        local.pop("up_bias").wait()
        row = jnp.concatenate([ub[...], jnp.zeros((1, 3 * UNITS), jnp.float32)], axis=1)
        row = pltpu.roll(jnp.broadcast_to(row, (8, 4 * UNITS)), UNITS * (2 * y_lo + core), 1)
        pieces[0] = row[:1]
        for i, chip in enumerate((twin, across, across_twin)):
            net.send(("piece", i), pieces.at[0], pieces.at[i + 1], chip)

    def bias_sum():
        net.wait(*(("piece", i) for i in range(3)))
        bias[0] = pieces[0] + pieces[1] + pieces[2] + pieces[3]
        for s, link in z_links.items():
            net.send(("bias", 1, s), bias.at[0], bias.at[slot(1, s)], link)

    def pass_bias(k, s):
        net.wait(("bias", k, s))
        net.send(("bias", k + 1, s), bias.at[slot(k, s)], bias.at[slot(k + 1, s)], z_links[s])

    def mlp_y():
        net.wait("up_lo")
        for s, link in z_links.items():
            net.send(("v", 1, s), block(0, 0, s, 1 - y_lo), block(0, 1, s, 1 - y_lo), link)

    def other(k, s):
        net.wait(("v", k, s))
        net.send(("v", k + 1, s), block(0, k, s, 1 - y_lo), block(0, k + 1, s, 1 - y_lo), z_links[s])

    def pass_on(p, k, s):
        net.wait((p, k, s))
        here = block(p, k, s, y_lo)
        if k < 3 or (k == 3 and (p % 2 == 0) == (s == 1)):
            net.send((p, k + 1, s), here, block(p, k + 1, s, y_lo), z_links[s])
        if p:
            net.send(("y", p, k, s), here, here, y_links[Y_LINK[p, s if k < 4 else 4]])

    def share_up(k, s):
        if k == 0:
            net.wait("up_lo", ("y", 1, 0, 1))
            local.pop("up").wait()
        elif k == 4:
            net.wait((0, 4, 1), (1, 4, -1), ("v", 4, 1), ("y", 1, 4, -1))
        else:
            net.wait((0, k, s), (1, k, s), ("v", k, s), ("y", 1, k, s))
        all_of_core = wu.at[slot(k, s), :, core]
        net.send(("share_up", k, s), all_of_core, all_of_core, twin)

    def share_down(k, s):
        if k == 0:
            net.wait(("y", 2, 0, 1), ("y", 3, 0, 1))
            local.pop("down").wait()
        elif k == 4:
            net.wait((2, 4, 1), (3, 4, -1), ("y", 2, 4, 1), ("y", 3, 4, -1))
        else:
            net.wait((2, k, s), (3, k, s), ("y", 2, k, s), ("y", 3, k, s))
        all_of_core = wd.at[slot(k, s), :, core]
        net.send(("share_down", k, s), all_of_core, all_of_core, twin)

    middle_rows = pl.ds(COLS, TOKENS)

    def embed():
        for name in ("patches", "embed", *(("vec", i) for i in range(4))):
            local.pop(name).wait()
        value = jnp.dot(patches[...], we[...], preferred_element_type=jnp.float32)
        value = (value + vecs[0][...]).astype(jnp.bfloat16)
        embedded[...] = value
        value = gelu(value.astype(jnp.float32)).astype(jnp.bfloat16)
        views[0, 1, COLS : COLS + TOKENS] = value
        act[...] = value.astype(jnp.float32)
        net.send("act", views.at[0, 1, middle_rows], views.at[1, 1, middle_rows], pair)
        for i in range(ROWS):
            first[i : i + 1] = act[i * COLS : i * COLS + 1]
            last[i : i + 1] = act[i * COLS + COLS - 1 : i * COLS + COLS]
        net.send("row_after", views.at[0, 1, pl.ds(TOKENS, COLS)], views.at[0, 1, pl.ds(0, COLS)], token(1, 0))
        net.send("row_before", views.at[0, 1, pl.ds(COLS, COLS)], views.at[0, 1, pl.ds(TOKENS + COLS, COLS)], token(-1, 0))
        for a in (0, 1, -1):
            net.send(("col_after", a), last, left.at[1 - a], token(a, 1))
            net.send(("col_before", a), first, right.at[1 - a], token(a, -1))

    def halo():
        net.wait("row_after", "row_before", *((n, a) for n in ("col_after", "col_before") for a in (0, 1, -1)))
        north, south = lat > 0, lat < 7
        none = jnp.zeros((6, WIDTH), jnp.float32)
        edges[0, :COLS] = jnp.where(north, views[0, 1, :COLS].astype(jnp.float32), 0.0).astype(jnp.bfloat16)
        edges[0, COLS : 2 * COLS] = jnp.where(south, views[0, 1, TOKENS + COLS :].astype(jnp.float32), 0.0).astype(jnp.bfloat16)
        for i, side in enumerate((left, right)):
            above = jnp.where(north, side[0, ROWS - 1 :], 0.0)
            below = jnp.where(south, side[2, :1], 0.0)
            column = jnp.concatenate([above, side[1], below, none], axis=0)
            edges[0, 2 * COLS + 16 * i : 2 * COLS + 16 * (i + 1)] = column.astype(jnp.bfloat16)
        net.send("edge", edges.at[0], edges.at[1], pair)
        frame(0)

    def frame_other():
        net.wait("act", "edge")
        frame(1)

    def frame(own_or_pair):
        place = lax.broadcasted_iota(jnp.int32, (COLS, WIDTH), 0)
        view, edge = views.at[own_or_pair], edges.at[own_or_pair]
        view[1, :COLS] = edge[:COLS]
        view[1, TOKENS + COLS :] = edge[COLS : 2 * COLS]
        columns = edge[2 * COLS :].astype(jnp.float32)
        for i in range(ROWS + 2):
            rows = slice(i * COLS, (i + 1) * COLS)
            middle = view[1, rows].astype(jnp.float32)
            view[0, rows] = jnp.where(place == 0, columns[i : i + 1], pltpu.roll(middle, 1, 0)).astype(jnp.bfloat16)
            after = jnp.where(place == COLS - 1, columns[16 + i : 17 + i], pltpu.roll(middle, COLS - 1, 0))
            view[2, rows] = after.astype(jnp.bfloat16)

    steps = (
        own, near, share, conv, swap, mlp, mlp_y, pass_on, other, share_up, share_down, embed, halo, frame_other, pass_bias, bias_sum,
    )
    for step, *args in ORDER:
        steps[step](*args)

    net.wait("swap")
    mine, theirs = total[:TOKENS], got[...].astype(jnp.float32)
    convolved = jnp.concatenate([jnp.where(y_hi == 0, mine, theirs), jnp.where(y_hi == 0, theirs, mine)], axis=1)
    mixed = (embedded[...].astype(jnp.float32) + convolved + vecs[1][...]).astype(jnp.bfloat16).astype(jnp.float32)
    center = jnp.mean(mixed, axis=1, keepdims=True)
    spread = jnp.mean((mixed - center) ** 2, axis=1, keepdims=True)
    normed[...] = ((mixed - center) * lax.rsqrt(spread + 1e-05) * vecs[2][...]).astype(jnp.bfloat16)
    summed[...] = mixed + vecs[3][...]

    def wait_shared(k, s):
        net.wait(("share_up", k, s), ("share_down", k, s), *([("bias", k, -1 if k == 4 else s)] if k else []))
        i = slot(k, s)
        biases[:, i * 4 * UNITS : (i + 1) * 4 * UNITS] = bias[i]

    ups, downs = wu.reshape(NZ * 4 * UNITS, WIDTH), wd.reshape(NZ * 4 * UNITS, WIDTH)

    def hidden_tiles(begin, end):
        for j in range(begin, end):
            units = slice(j * TILE, (j + 1) * TILE)
            hidden[:, units] = gelu(nt(normed[...], ups[units]) + biases[:, units]).astype(jnp.bfloat16)
        units = slice(begin * TILE, end * TILE)
        return jnp.dot(hidden[:, units], downs[units], preferred_element_type=jnp.float32)

    for k, s in ((0, 1), (1, 1), (1, -1), (2, 1), (2, -1), (3, 1), (3, -1)):
        wait_shared(k, s)
    summed[...] += hidden_tiles(0, 10)
    wait_shared(4, 1)
    out_ref[...] = (summed[...] + hidden_tiles(10, 12)).astype(jnp.bfloat16)
    net.finish()
    assert len(net.made) == COPIES


def body(patches, embed_weight, embed_bias, conv_weight, conv_bias, norm_gain, up_weight, up_bias, down_weight, down_bias):
    rows, cols, inputs = patches.shape
    bf16, f32 = jnp.bfloat16, jnp.float32
    out = pl.pallas_call(
        kernel,
        out_shape=jax.ShapeDtypeStruct((TOKENS, WIDTH), bf16),
        in_specs=[pl.BlockSpec(memory_space=pl.ANY)] * 10,
        out_specs=pl.BlockSpec(memory_space=pltpu.VMEM),
        scratch_shapes=[
            pltpu.VMEM((TAPS, NX, 2, HALF, WIDTH), bf16),
            pltpu.VMEM((NZ, 2, 2, UNITS, WIDTH), bf16),
            pltpu.VMEM((NZ, 2, 2, UNITS, WIDTH), bf16),
            pltpu.VMEM((4, 1, 4 * UNITS), f32),
            pltpu.VMEM((NZ, 1, 4 * UNITS), f32),
            pltpu.VMEM((TOKENS, inputs), bf16),
            pltpu.VMEM((inputs, WIDTH), bf16),
            *[pltpu.VMEM((WIDTH,), f32)] * 4,
            pltpu.VMEM((1, UNITS), f32),
            pltpu.VMEM((TOKENS, WIDTH), f32),
            pltpu.VMEM((TOKENS, WIDTH), bf16),
            pltpu.VMEM((2, 3, TOKENS + 2 * COLS, WIDTH), bf16),
            pltpu.VMEM((3, ROWS, WIDTH), f32),
            pltpu.VMEM((3, ROWS, WIDTH), f32),
            pltpu.VMEM((ROWS, WIDTH), f32),
            pltpu.VMEM((ROWS, WIDTH), f32),
            pltpu.VMEM((2, 2 * COLS + 32, WIDTH), bf16),
            pltpu.VMEM((2 * TOKENS, OUT), f32),
            pltpu.VMEM((TOKENS, OUT), bf16),
            pltpu.VMEM((TOKENS, OUT), bf16),
            pltpu.VMEM((TOKENS, WIDTH), f32),
            pltpu.VMEM((TOKENS, WIDTH), bf16),
            pltpu.VMEM((TOKENS, NZ * 4 * UNITS), bf16),
            pltpu.VMEM((1, NZ * 4 * UNITS), f32),
            pltpu.SemaphoreType.DMA((10,)),
            pltpu.SemaphoreType.DMA((1,)),
            pltpu.SemaphoreType.DMA((COPIES,)),
        ],
        compiler_params=pltpu.CompilerParams(collective_id=0, has_side_effects=True, vmem_limit_bytes=56 << 20),
        cost_estimate=pl.CostEstimate(flops=5_570_000_000, bytes_accessed=5_000_000, transcendentals=1_000_000),
        name="block",
    )(
        patches.reshape(TOKENS, inputs),
        embed_weight,
        jnp.swapaxes(conv_weight, 2, 3).reshape(TAPS, 2, HALF, WIDTH),
        up_weight.T,
        down_weight.T,
        embed_bias,
        conv_bias,
        norm_gain,
        up_bias,
        down_bias,
    )
    return out.reshape(rows, cols, WIDTH)


def solution(mesh):
    in_specs = (
        P("lat", "lon", None),
        P(),
        P(),
        P(None, None, None, "lat"),
        P(),
        P(),
        P(None, "lon"),
        P(None, "lon"),
        P(None, "lon"),
        P(),
    )
    return jax.shard_map(body, mesh=mesh, in_specs=in_specs, out_specs=P("lat", "lon", None), check_vma=False)
```

```python
import jax
import jax.numpy as jnp
from jax import lax
from jax.experimental import pallas as pl
from jax.experimental.pallas import tpu as pltpu
from jax.sharding import PartitionSpec as P

MESH = pl.DeviceIdType.MESH
NX, NZ = 4, 8
ROWS, COLS, WIDTH, UNITS = 8, 32, 768, 96
TOKENS, HALF, TILE = ROWS * COLS, UNITS // 2, 256
OUT = WIDTH // 2
TAPS = 9
COPIES = 133
PARTS = range(4)
OWN, NEAR, SHARE, CONV, SWAP, MLP, MLP_Y, PASS, OTHER, SHARE_UP, SHARE_DOWN, EMBED, HALO, FRAME, BIAS, BIAS_SUM = range(16)
WAY = (1, -1, 1, -1, 1, -1, 1, -1, 1)
Y_LINK = {(2, 0): 0, (2, 4): 0, (2, -1): 1, (2, 1): 0, (3, 0): 0, (3, 4): 0, (3, -1): 0, (3, 1): 1, (1, 0): 1, (1, 4): 0, (1, -1): 0, (1, 1): 0}
ORDER = (
    (OWN, 0), (OWN, 1), (MLP,), (EMBED,), (OWN, 2), (OWN, 3), (NEAR, 0), (MLP_Y,), (PASS, 0, 1, 1), (PASS, 0, 1, -1),
    (SHARE_UP, 0, 1), (OWN, 4), (NEAR, 1), (PASS, 1, 1, 1), (PASS, 1, 1, -1), (HALO,), (OWN, 5), (SHARE_DOWN, 0, 1),
    (PASS, 2, 1, 1), (PASS, 2, 1, -1), (BIAS_SUM,), (NEAR, 2), (OWN, 6), (NEAR, 3), (PASS, 3, 1, 1), (PASS, 3, 1, -1),
    (OWN, 7), (OTHER, 1, 1), (OTHER, 1, -1), (SHARE_UP, 1, 1), (SHARE_UP, 1, -1), (SHARE, 0), (OWN, 8), (SHARE, 1),
    (PASS, 0, 2, 1), (PASS, 0, 2, -1), (NEAR, 4), (NEAR, 5), (PASS, 1, 2, 1), (PASS, 1, 2, -1), (PASS, 2, 2, 1),
    (PASS, 2, 2, -1), (BIAS, 1, 1), (BIAS, 1, -1), (FRAME,), (SHARE, 2), (CONV, 0), (PASS, 3, 2, 1), (PASS, 3, 2, -1),
    (SHARE, 3), (CONV, 1), (NEAR, 6), (SHARE_DOWN, 1, -1), (CONV, 2), (NEAR, 7), (OTHER, 2, 1), (OTHER, 2, -1),
    (SHARE_UP, 2, -1), (SHARE_UP, 2, 1), (CONV, 3), (SHARE_DOWN, 1, 1), (PASS, 0, 3, 1), (NEAR, 8), (SHARE, 5),
    (SHARE_DOWN, 2, -1), (PASS, 1, 3, 1), (PASS, 1, 3, -1), (SHARE_DOWN, 2, 1), (SHARE, 4), (CONV, 5),
    (PASS, 2, 3, 1), (BIAS, 2, 1), (PASS, 2, 3, -1), (BIAS, 2, -1), (SHARE, 7), (SHARE, 6), (CONV, 4),
    (PASS, 3, 3, 1), (PASS, 3, 3, -1), (CONV, 7), (SHARE, 8), (CONV, 6), (OTHER, 3, 1), (SHARE_UP, 3, 1),
    (SHARE_UP, 3, -1), (CONV, 8), (SWAP,), (PASS, 1, 4, -1), (SHARE_DOWN, 3, 1), (BIAS, 3, -1), (SHARE_DOWN, 3, -1),
    (PASS, 2, 4, 1), (PASS, 3, 4, -1), (SHARE_UP, 4, 1), (SHARE_DOWN, 4, 1),
)


def slot(k, s):
    return 7 if k == 4 else 0 if k == 0 else 2 * k - (s == 1)


def gelu(v):
    return 0.5 * v * (1.0 + jnp.tanh(0.7978845608028654 * (v + 0.044715 * (v * v * v))))


def nt(a, b):
    return lax.dot_general(a, b, (((1,), (1,)), ((), ())), preferred_element_type=jnp.float32)


class Copies:
    def __init__(self, send_sem, recv_sem):
        self.send_sem, self.recv_sem = send_sem, recv_sem
        self.made, self.arrived = {}, set()

    def send(self, name, src, dst, device):
        i = len(self.made)
        copy = pltpu.make_async_remote_copy(
            src_ref=src, dst_ref=dst, send_sem=self.send_sem.at[0], recv_sem=self.recv_sem.at[i],
            device_id=device, device_id_type=MESH,
        )
        copy.start()
        self.made[name] = copy

    def wait(self, *names):
        for name in names:
            if name not in self.arrived:
                self.arrived.add(name)
                self.made[name].wait_recv()

    def finish(self):
        for name, copy in self.made.items():
            self.wait(name)
        for copy in self.made.values():
            copy.wait_send()


def kernel(
    patches_hbm, embed_hbm, conv_hbm, up_hbm, down_hbm, embed_bias_hbm, conv_bias_hbm, gain_hbm, up_bias_hbm, down_bias_hbm,
    out_ref,
    wc, wu, wd, pieces, bias, patches, we, v0, v1, v2, v3, ub, act, embedded, views, left, right, first, last, edges, total, give, got,
    summed, normed, hidden, biases, done, local_sem, send_sem, recv_sem,
):
    vecs = (v0, v1, v2, v3)
    lon, lat = lax.axis_index("lon"), lax.axis_index("lat")
    z, y_lo, core = lon // 4, (lon // 2) % 2, lon % 2
    y_hi, x = lat // NX, lat % NX

    def device(x, y_hi, z, y_lo, core):
        return {"lon": z * 4 + y_lo * 2 + core, "lat": y_hi * NX + x}

    def along_x(d):
        return (x + d + NX) % NX

    def along_z(d):
        return (z + d + NZ) % NZ

    x_links = {1: device(along_x(1), y_hi, z, y_lo, core), -1: device(along_x(-1), y_hi, z, y_lo, core)}
    z_links = {1: device(x, y_hi, along_z(1), y_lo, core), -1: device(x, y_hi, along_z(-1), y_lo, core)}
    pair = device(x, 1 - y_hi, z, 1 - y_lo, core)
    across = device(x, y_hi, z, 1 - y_lo, core)
    across_twin = device(x, y_hi, z, 1 - y_lo, 1 - core)
    y_links = (across, pair)
    twin = device(x, y_hi, z, y_lo, 1 - core)

    def token(dlat, dlon):
        return {"lon": (lon + dlon + 32) % 32, "lat": (lat + dlat + 8) % 8}

    around = [token(a, b) for a in (-1, 0, 1) for b in (-1, 0, 1) if a or b]

    local = {}

    def fetch(name, src, dst):
        local[name] = pltpu.make_async_copy(src, dst, local_sem.at[len(local)])
        local[name].start()

    fetch("patches", patches_hbm, patches)
    fetch("embed", embed_hbm, we)
    for i, vec in enumerate((embed_bias_hbm, conv_bias_hbm, gain_hbm, down_bias_hbm)):
        fetch(("vec", i), vec, vecs[i])
    fetch("up_bias", up_bias_hbm, ub)
    fetch("conv", conv_hbm.at[:, core], wc.at[:, x, core])
    fetch("up", up_hbm, wu.at[0, y_lo, core])
    fetch("down", down_hbm, wd.at[0, y_lo, core])

    barrier = pltpu.get_barrier_semaphore()
    partners = [*x_links.values(), *z_links.values(), pair, across, twin, across_twin] + around
    for partner in partners:
        pl.semaphore_signal(barrier, inc=1, device_id=partner, device_id_type=MESH)
    pl.semaphore_wait(barrier, len(partners))

    net = Copies(send_sem, recv_sem)
    taps = wc.reshape(TAPS, OUT, WIDTH)

    def own(t):
        for d, link in x_links.items():
            net.send(("own_x", t, d), conv_hbm.at[t, core], wc.at[t, x, core], link)

    def near(t):
        d = WAY[t]
        net.wait(("own_x", t, d))
        block = wc.at[t, along_x(-d), core]
        net.send(("far", t), block, block, x_links[d])

    def share(t):
        net.wait(("own_x", t, 1), ("own_x", t, -1), ("far", t))
        if "conv" in local:
            local.pop("conv").wait()
        block = wc.at[t, :, core]
        net.send(("share", t), block, block, twin)

    def conv(t):
        net.wait(("share", t))
        a, b = t // 3, t % 3
        rows = slice(a * COLS, a * COLS + TOKENS)
        term = nt(jnp.concatenate([views[0, b, rows], views[1, b, rows]]), taps[t])
        total[...] = term if t == 0 else total[...] + term

    def swap():
        give[...] = total[TOKENS:].astype(jnp.bfloat16)
        net.send("swap", give, got, pair)

    def half(array, p):
        return array.at[pl.ds(p % 2 * HALF, HALF)]

    def block(p, k, s, lo):
        return half((wu if p < 2 else wd).at[slot(k, s), lo, core], p)

    def mlp():
        given = (up_hbm, up_hbm, down_hbm, down_hbm)
        net.send("up_lo", half(up_hbm, 0), block(0, 0, 1, y_lo), across)
        for p in PARTS:
            for s, link in z_links.items():
                net.send((p, 1, s), half(given[p], p), block(p, 1, s, y_lo), link)
        for p in PARTS[1:]:
            net.send(("y", p, 0, 1), half(given[p], p), block(p, 0, 1, y_lo), y_links[Y_LINK[p, 0]])
        local.pop("up_bias").wait()
        row = jnp.concatenate([ub[...], jnp.zeros((1, 3 * UNITS), jnp.float32)], axis=1)
        row = pltpu.roll(jnp.broadcast_to(row, (8, 4 * UNITS)), UNITS * (2 * y_lo + core), 1)
        pieces[0] = row[:1]
        for i, chip in enumerate((twin, across, across_twin)):
            net.send(("piece", i), pieces.at[0], pieces.at[i + 1], chip)

    def bias_sum():
        net.wait(*(("piece", i) for i in range(3)))
        bias[0] = pieces[0] + pieces[1] + pieces[2] + pieces[3]
        for s, link in z_links.items():
            net.send(("bias", 1, s), bias.at[0], bias.at[slot(1, s)], link)

    def pass_bias(k, s):
        net.wait(("bias", k, s))
        net.send(("bias", k + 1, s), bias.at[slot(k, s)], bias.at[slot(k + 1, s)], z_links[s])

    def mlp_y():
        net.wait("up_lo")
        for s, link in z_links.items():
            net.send(("v", 1, s), block(0, 0, s, 1 - y_lo), block(0, 1, s, 1 - y_lo), link)

    def other(k, s):
        net.wait(("v", k, s))
        net.send(("v", k + 1, s), block(0, k, s, 1 - y_lo), block(0, k + 1, s, 1 - y_lo), z_links[s])

    def pass_on(p, k, s):
        net.wait((p, k, s))
        here = block(p, k, s, y_lo)
        if k < 3 or (k == 3 and (p % 2 == 0) == (s == 1)):
            net.send((p, k + 1, s), here, block(p, k + 1, s, y_lo), z_links[s])
        if p:
            net.send(("y", p, k, s), here, here, y_links[Y_LINK[p, s if k < 4 else 4]])

    def share_up(k, s):
        if k == 0:
            net.wait("up_lo", ("y", 1, 0, 1))
            local.pop("up").wait()
        elif k == 4:
            net.wait((0, 4, 1), (1, 4, -1), ("v", 4, 1), ("y", 1, 4, -1))
        else:
            net.wait((0, k, s), (1, k, s), ("v", k, s), ("y", 1, k, s))
        all_of_core = wu.at[slot(k, s), :, core]
        net.send(("share_up", k, s), all_of_core, all_of_core, twin)

    def share_down(k, s):
        if k == 0:
            net.wait(("y", 2, 0, 1), ("y", 3, 0, 1))
            local.pop("down").wait()
        elif k == 4:
            net.wait((2, 4, 1), (3, 4, -1), ("y", 2, 4, 1), ("y", 3, 4, -1))
        else:
            net.wait((2, k, s), (3, k, s), ("y", 2, k, s), ("y", 3, k, s))
        all_of_core = wd.at[slot(k, s), :, core]
        net.send(("share_down", k, s), all_of_core, all_of_core, twin)

    middle_rows = pl.ds(COLS, TOKENS)

    def embed():
        for name in ("patches", "embed", *(("vec", i) for i in range(4))):
            local.pop(name).wait()
        value = jnp.dot(patches[...], we[...], preferred_element_type=jnp.float32)
        value = (value + vecs[0][...]).astype(jnp.bfloat16)
        embedded[...] = value
        value = gelu(value.astype(jnp.float32)).astype(jnp.bfloat16)
        views[0, 1, COLS : COLS + TOKENS] = value
        act[...] = value.astype(jnp.float32)
        net.send("act", views.at[0, 1, middle_rows], views.at[1, 1, middle_rows], pair)
        for i in range(ROWS):
            first[i : i + 1] = act[i * COLS : i * COLS + 1]
            last[i : i + 1] = act[i * COLS + COLS - 1 : i * COLS + COLS]
        net.send("row_after", views.at[0, 1, pl.ds(TOKENS, COLS)], views.at[0, 1, pl.ds(0, COLS)], token(1, 0))
        net.send("row_before", views.at[0, 1, pl.ds(COLS, COLS)], views.at[0, 1, pl.ds(TOKENS + COLS, COLS)], token(-1, 0))
        for a in (0, 1, -1):
            net.send(("col_after", a), last, left.at[1 - a], token(a, 1))
            net.send(("col_before", a), first, right.at[1 - a], token(a, -1))

    def halo():
        net.wait("row_after", "row_before", *((n, a) for n in ("col_after", "col_before") for a in (0, 1, -1)))
        north, south = lat > 0, lat < 7
        none = jnp.zeros((6, WIDTH), jnp.float32)
        edges[0, :COLS] = jnp.where(north, views[0, 1, :COLS].astype(jnp.float32), 0.0).astype(jnp.bfloat16)
        edges[0, COLS : 2 * COLS] = jnp.where(south, views[0, 1, TOKENS + COLS :].astype(jnp.float32), 0.0).astype(jnp.bfloat16)
        for i, side in enumerate((left, right)):
            above = jnp.where(north, side[0, ROWS - 1 :], 0.0)
            below = jnp.where(south, side[2, :1], 0.0)
            column = jnp.concatenate([above, side[1], below, none], axis=0)
            edges[0, 2 * COLS + 16 * i : 2 * COLS + 16 * (i + 1)] = column.astype(jnp.bfloat16)
        net.send("edge", edges.at[0], edges.at[1], pair)
        frame(0)

    def frame_other():
        net.wait("act", "edge")
        frame(1)

    def frame(own_or_pair):
        place = lax.broadcasted_iota(jnp.int32, (COLS, WIDTH), 0)
        view, edge = views.at[own_or_pair], edges.at[own_or_pair]
        view[1, :COLS] = edge[:COLS]
        view[1, TOKENS + COLS :] = edge[COLS : 2 * COLS]
        columns = edge[2 * COLS :].astype(jnp.float32)
        for i in range(ROWS + 2):
            rows = slice(i * COLS, (i + 1) * COLS)
            middle = view[1, rows].astype(jnp.float32)
            view[0, rows] = jnp.where(place == 0, columns[i : i + 1], pltpu.roll(middle, 1, 0)).astype(jnp.bfloat16)
            after = jnp.where(place == COLS - 1, columns[16 + i : 17 + i], pltpu.roll(middle, COLS - 1, 0))
            view[2, rows] = after.astype(jnp.bfloat16)

    steps = (
        own, near, share, conv, swap, mlp, mlp_y, pass_on, other, share_up, share_down, embed, halo, frame_other, pass_bias, bias_sum,
    )
    for step, *args in ORDER:
        steps[step](*args)

    net.wait("swap")
    mine, theirs = total[:TOKENS], got[...].astype(jnp.float32)
    convolved = jnp.concatenate([jnp.where(y_hi == 0, mine, theirs), jnp.where(y_hi == 0, theirs, mine)], axis=1)
    mixed = (embedded[...].astype(jnp.float32) + convolved + vecs[1][...]).astype(jnp.bfloat16).astype(jnp.float32)
    center = jnp.mean(mixed, axis=1, keepdims=True)
    spread = jnp.mean((mixed - center) ** 2, axis=1, keepdims=True)
    normed[...] = ((mixed - center) * lax.rsqrt(spread + 1e-05) * vecs[2][...]).astype(jnp.bfloat16)
    summed[...] = mixed + vecs[3][...]

    def wait_shared(k, s):
        net.wait(("share_up", k, s), ("share_down", k, s), *([("bias", k, -1 if k == 4 else s)] if k else []))
        i = slot(k, s)
        biases[:, i * 4 * UNITS : (i + 1) * 4 * UNITS] = bias[i]

    ups, downs = wu.reshape(NZ * 4 * UNITS, WIDTH), wd.reshape(NZ * 4 * UNITS, WIDTH)

    def hidden_tiles(begin, end):
        for j in range(begin, end):
            units = slice(j * TILE, (j + 1) * TILE)
            hidden[:, units] = gelu(nt(normed[...], ups[units]) + biases[:, units]).astype(jnp.bfloat16)
        units = slice(begin * TILE, end * TILE)
        return jnp.dot(hidden[:, units], downs[units], preferred_element_type=jnp.float32)

    for k, s in ((0, 1), (1, 1), (1, -1), (2, 1), (2, -1), (3, 1), (3, -1)):
        wait_shared(k, s)
    summed[...] += hidden_tiles(0, 10)
    wait_shared(4, 1)
    for j in (10, 11):
        units = slice(j * TILE, (j + 1) * TILE)
        hidden[:, units] = gelu(nt(normed[...], ups[units]) + biases[:, units]).astype(jnp.bfloat16)
    results = []
    for i in range(2):
        rows, units = pl.ds(i * TOKENS // 2, TOKENS // 2), slice(10 * TILE, 12 * TILE)
        last_term = jnp.dot(hidden[rows, units], downs[units], preferred_element_type=jnp.float32)
        done[rows] = (summed[rows] + last_term).astype(jnp.bfloat16)
        results.append(pltpu.make_async_copy(done.at[rows], out_ref.at[rows], local_sem.at[i]))
        results[i].start()
    net.finish()
    for result in results:
        result.wait()
    assert len(net.made) == COPIES


def body(patches, embed_weight, embed_bias, conv_weight, conv_bias, norm_gain, up_weight, up_bias, down_weight, down_bias):
    rows, cols, inputs = patches.shape
    bf16, f32 = jnp.bfloat16, jnp.float32
    out = pl.pallas_call(
        kernel,
        out_shape=jax.ShapeDtypeStruct((TOKENS, WIDTH), bf16),
        in_specs=[pl.BlockSpec(memory_space=pl.ANY)] * 10,
        out_specs=pl.BlockSpec(memory_space=pl.ANY),
        scratch_shapes=[
            pltpu.VMEM((TAPS, NX, 2, HALF, WIDTH), bf16),
            pltpu.VMEM((NZ, 2, 2, UNITS, WIDTH), bf16),
            pltpu.VMEM((NZ, 2, 2, UNITS, WIDTH), bf16),
            pltpu.VMEM((4, 1, 4 * UNITS), f32),
            pltpu.VMEM((NZ, 1, 4 * UNITS), f32),
            pltpu.VMEM((TOKENS, inputs), bf16),
            pltpu.VMEM((inputs, WIDTH), bf16),
            *[pltpu.VMEM((WIDTH,), f32)] * 4,
            pltpu.VMEM((1, UNITS), f32),
            pltpu.VMEM((TOKENS, WIDTH), f32),
            pltpu.VMEM((TOKENS, WIDTH), bf16),
            pltpu.VMEM((2, 3, TOKENS + 2 * COLS, WIDTH), bf16),
            pltpu.VMEM((3, ROWS, WIDTH), f32),
            pltpu.VMEM((3, ROWS, WIDTH), f32),
            pltpu.VMEM((ROWS, WIDTH), f32),
            pltpu.VMEM((ROWS, WIDTH), f32),
            pltpu.VMEM((2, 2 * COLS + 32, WIDTH), bf16),
            pltpu.VMEM((2 * TOKENS, OUT), f32),
            pltpu.VMEM((TOKENS, OUT), bf16),
            pltpu.VMEM((TOKENS, OUT), bf16),
            pltpu.VMEM((TOKENS, WIDTH), f32),
            pltpu.VMEM((TOKENS, WIDTH), bf16),
            pltpu.VMEM((TOKENS, NZ * 4 * UNITS), bf16),
            pltpu.VMEM((1, NZ * 4 * UNITS), f32),
            pltpu.VMEM((TOKENS, WIDTH), bf16),
            pltpu.SemaphoreType.DMA((10,)),
            pltpu.SemaphoreType.DMA((1,)),
            pltpu.SemaphoreType.DMA((COPIES,)),
        ],
        compiler_params=pltpu.CompilerParams(collective_id=0, has_side_effects=True, vmem_limit_bytes=56 << 20),
        cost_estimate=pl.CostEstimate(flops=5_570_000_000, bytes_accessed=5_000_000, transcendentals=1_000_000),
        name="block",
    )(
        patches.reshape(TOKENS, inputs),
        embed_weight,
        jnp.swapaxes(conv_weight, 2, 3).reshape(TAPS, 2, HALF, WIDTH),
        up_weight.T,
        down_weight.T,
        embed_bias,
        conv_bias,
        norm_gain,
        up_bias,
        down_bias,
    )
    return out.reshape(rows, cols, WIDTH)


def solution(mesh):
    in_specs = (
        P("lat", "lon", None),
        P(),
        P(),
        P(None, None, None, "lat"),
        P(),
        P(),
        P(None, "lon"),
        P(None, "lon"),
        P(None, "lon"),
        P(),
    )
    return jax.shard_map(body, mesh=mesh, in_specs=in_specs, out_specs=P("lat", "lon", None), check_vma=False)
```
